32 devices in a mesh: groups: 2 (over y), ctx: 4 (over z), tp: 2 (over x), kv: 2 (over core).
Axes of the slice: x: 2, y: 2, z: 4, core: 2. Of those that a mesh axis runs over, the one named last changes fastest.
Arguments:
- queries: bfloat16 [2048, 8192], P(('groups', 'ctx'), ('tp', 'kv')), parts along dimension 0, may hold values from -8 to 8
- key_matrix: bfloat16 [2048, 1024], P(('groups', 'ctx'), 'tp'), parts along dimension 0, may hold values from -8 to 8
- value_matrix: bfloat16 [2048, 1024], P(('groups', 'ctx'), 'tp'), parts along dimension 0, may hold values from -6 to 6
- out_grad: bfloat16 [2048, 8192], P(('groups', 'ctx'), ('tp', 'kv')), parts along dimension 0, may hold values from -6 to 6
- segments: int32 [2048], P(('groups', 'ctx')), parts along dimension 0, may hold values from 0 to 15, never falling along the last dimension, each value on 1 to 512 neighbouring positions
Outputs:
- query_grad: bfloat16 [2048, 8192], P(('groups', 'ctx'), ('tp', 'kv')), parts along dimension 0
- key_gradient: bfloat16 [2048, 1024], P(('groups', 'ctx'), 'tp'), parts along dimension 0
- value_gradient: bfloat16 [2048, 1024], P(('groups', 'ctx'), 'tp'), parts along dimension 0
The draws below stay inside these ranges and needn't reach their ends.
There are 2 independent parts, one for each index of `groups`. The reference program is written for one: setup_inputs(seed, part) draws one part's arguments, and reference() takes and returns one part's arrays. A program takes and returns all parts, laid end to end along the dimension named above; each array names one. Nothing has to cross between parts.
Inputs may be any that keep to these rules, and one draw needn't show every extreme that they name: `segments`: document numbers never fall along the sequence; each of the 16 documents has 1 or more positions and one document holds exactly half of the 1024 positions.
All inputs are finite; a program needn't handle non-finite values.
Results may differ from the reference program's by a relative error of at most 0.011.
Values may be sent and summed in bfloat16 or wider, within the bound.
No kernel may reach another device: no remote copies, remote signals or barrier semaphores. Data moves between devices by JAX's collectives and lax.ppermute only.
A program may use at most 64 MiB of HBM per device.

```python
import math
import jax
import jax.numpy as jnp
import numpy as np
from jax import lax

QUERY_HEADS = 64
KEY_VALUE_HEADS = 8
HEAD_SIZE = 128
DOCS = 16
PACKED_LENGTH = 1024


def draw_key_matrix(key, part):
    output_rows = jnp.clip(jax.random.normal(jax.random.fold_in(key, 11), (PACKED_LENGTH, KEY_VALUE_HEADS, HEAD_SIZE), jnp.float32), -6.0, 6.0)
    return output_rows.reshape(PACKED_LENGTH, KEY_VALUE_HEADS * HEAD_SIZE).astype(jnp.bfloat16)


def draw_queries(key, part):
    output_rows = jnp.clip(jax.random.normal(jax.random.fold_in(key, 13), (PACKED_LENGTH, QUERY_HEADS, HEAD_SIZE), jnp.float32), -6.0, 6.0)
    return output_rows.reshape(PACKED_LENGTH, QUERY_HEADS * HEAD_SIZE).astype(jnp.bfloat16)


def levels(rng, shape, split, least, top_value):
    level, own = 1.0, jax.random.fold_in(rng, 6)
    for dim, blocks in split:
        draws = jnp.exp(jax.random.uniform(jax.random.fold_in(own, dim), (blocks,), jnp.float32, least / len(split), top_value / len(split)))
        level = level * jnp.repeat(draws, shape[dim] // blocks).reshape([-1 if axis == dim else 1 for axis in range(len(shape))])
    return level


def split_up(number_of, total, bound, slope):
    loads = [(1 << 20) // math.isqrt(rank ** slope) + 1 for rank in range(2, number_of + 1)]
    spare, given = total - bound - (number_of - 1), [1] * (number_of - 1)
    while spare > 0:
        movable = [i for i in range(number_of - 1) if given[i] < bound]
        whole, budget = sum([loads[i] for i in movable]), spare
        for i in movable:
            addition = min(bound - given[i], max(1, budget * loads[i] // whole), spare)
            given[i] = given[i] + addition
            spare = spare - addition
    return np.array([bound] + given)


def ragged(rng, number_of, total, reach, lean):
    if number_of == 2:
        one = jax.random.randint(rng, (), max(1, total - reach), min(reach, total - 1) + 1)
        return jnp.stack([one, total - one])
    sizes = jnp.asarray(split_up(number_of, total, reach, lean), jnp.int32)
    couples = (number_of - 1) // 2
    giver, receiver = sizes[1:1 + 2 * couples:2], sizes[2:2 + 2 * couples:2]
    margin = jnp.minimum(giver - 1, reach - receiver)
    moved = jax.random.randint(jax.random.fold_in(rng, 1), (couples,), 0, 1 << 20) % (margin + 1)
    sizes = sizes.at[1:1 + 2 * couples:2].set(giver - moved).at[2:2 + 2 * couples:2].set(receiver + moved)
    return sizes[jax.random.permutation(jax.random.fold_in(rng, 2), number_of)]


def centred(rng, shape, width, bound, pieces=(), kind=jnp.bfloat16):
    array = jax.random.normal(rng, shape, jnp.float32) * width
    if len(pieces) > 0:
        array = levels(rng, shape, pieces, -0.22, 0.18) * array
    return jnp.clip(array, min=-bound, max=bound).astype(kind)


def setup_inputs(seed: int = 0, part: int = 0) -> dict:
    seeds = jax.random.split(jax.random.key(seed), 6)
    part_splits = jax.random.split(jax.random.fold_in(seeds[5], part), 6)
    queries = draw_queries(jax.random.fold_in(jax.random.fold_in(seeds[5], part), 71), part)
    key_matrix = draw_key_matrix(jax.random.fold_in(jax.random.fold_in(seeds[5], part), 71), part)
    value_matrix = centred(part_splits[2], (PACKED_LENGTH, KEY_VALUE_HEADS * HEAD_SIZE), 1.0, 6.0, ((0, 4), (1, 2)))
    out_grad = centred(part_splits[3], (PACKED_LENGTH, QUERY_HEADS * HEAD_SIZE), 1.0, 6.0, ((0, 4), (1, 4)))
    segments = jnp.searchsorted(jnp.cumsum(ragged(part_splits[4], DOCS, PACKED_LENGTH, PACKED_LENGTH // 2, 2)), jnp.arange(PACKED_LENGTH), side="right").astype(jnp.int32)
    return {"queries": queries, "key_matrix": key_matrix, "value_matrix": value_matrix, "out_grad": out_grad, "segments": segments}


def head_backward(inputs, segments, logit_scale):
    q_head, g_head, k_head, v_head = inputs
    span_length = q_head.shape[0]
    parts_count = 8
    rows_each = span_length // parts_count
    position = jnp.arange(span_length, dtype=jnp.int32)
    query_pieces = []
    key_total = jnp.zeros((span_length, HEAD_SIZE), jnp.float32)
    value_total = jnp.zeros((span_length, HEAD_SIZE), jnp.float32)
    for piece_index in range(parts_count):
        row_first = piece_index * rows_each
        row_end = row_first + rows_each
        q_rows = q_head[row_first:row_end]
        g_rows = g_head[row_first:row_end]
        k_rows = k_head[:row_end]
        v_rows = v_head[:row_end]
        allowed = (segments[row_first:row_end, None] == segments[None, :row_end]) & (position[None, :row_end] <= position[row_first:row_end, None])
        logits = jnp.dot(q_rows, k_rows.T, preferred_element_type=jnp.float32) * logit_scale
        masked_logits = jnp.where(allowed, logits, -jnp.inf)
        row_peak = jnp.max(masked_logits, axis=1, keepdims=True)
        totals = jnp.sum(jnp.where(allowed, jnp.exp(logits - row_peak), 0.0), axis=1, keepdims=True)
        log_total = row_peak + jnp.log(totals)
        probs = jnp.where(allowed, jnp.exp(logits - log_total), 0.0)
        dprobs = jnp.dot(g_rows, v_rows.T, preferred_element_type=jnp.float32)
        deltas = jnp.sum(probs * dprobs, axis=1, keepdims=True)
        dlogits = probs * (dprobs - deltas)
        probs_low = probs.astype(jnp.bfloat16)
        dlogits_low = dlogits.astype(jnp.bfloat16)
        query_pieces.append(jnp.dot(dlogits_low, k_rows, preferred_element_type=jnp.float32) * logit_scale)
        key_piece = jnp.dot(dlogits_low.T, q_rows, preferred_element_type=jnp.float32)
        value_piece = jnp.dot(probs_low.T, g_rows, preferred_element_type=jnp.float32)
        key_total = key_total + jnp.pad(key_piece, ((0, span_length - row_end), (0, 0)))
        value_total = value_total + jnp.pad(value_piece, ((0, span_length - row_end), (0, 0)))
    return jnp.concatenate(query_pieces, axis=0), key_total, value_total


def reference(queries, key_matrix, value_matrix, out_grad, segments):
    span_length = queries.shape[0]
    group_width = QUERY_HEADS // KEY_VALUE_HEADS
    logit_scale = HEAD_SIZE ** -0.5
    q_heads = queries.reshape(span_length, QUERY_HEADS, HEAD_SIZE).transpose(1, 0, 2)
    g_heads = out_grad.reshape(span_length, QUERY_HEADS, HEAD_SIZE).transpose(1, 0, 2)
    key_head_list = jnp.repeat(key_matrix.reshape(span_length, KEY_VALUE_HEADS, HEAD_SIZE).transpose(1, 0, 2), group_width, axis=0)
    value_head_list = jnp.repeat(value_matrix.reshape(span_length, KEY_VALUE_HEADS, HEAD_SIZE).transpose(1, 0, 2), group_width, axis=0)

    def one_head(inputs):
        return head_backward(inputs, segments, logit_scale)

    query_parts, key_portions, value_portions = lax.map(one_head, (q_heads, g_heads, key_head_list, value_head_list))
    query_grad = query_parts.transpose(1, 0, 2).reshape(span_length, QUERY_HEADS * HEAD_SIZE).astype(jnp.bfloat16)
    key_total_sum = jnp.sum(key_portions.reshape(KEY_VALUE_HEADS, group_width, span_length, HEAD_SIZE), axis=1) * logit_scale
    value_total_sum = jnp.sum(value_portions.reshape(KEY_VALUE_HEADS, group_width, span_length, HEAD_SIZE), axis=1)
    key_gradient = key_total_sum.transpose(1, 0, 2).reshape(span_length, KEY_VALUE_HEADS * HEAD_SIZE).astype(jnp.bfloat16)
    value_gradient = value_total_sum.transpose(1, 0, 2).reshape(span_length, KEY_VALUE_HEADS * HEAD_SIZE).astype(jnp.bfloat16)
    return query_grad, key_gradient, value_gradient
```

```python
import functools
import jax
import jax.numpy as jnp
from jax import lax
from jax.experimental import pallas as pl
from jax.experimental.pallas import tpu as pltpu
from jax.sharding import PartitionSpec as P

QUERY_HEADS = 64
KEY_VALUE_HEADS = 8
HEAD_SIZE = 128
SEGMENT_ROWS = 16
TILE = 32
HINT = 0.2
AHEAD = 3
FILL_LOW = -1e30
LOG2_E = 1.4426950408889634
VMEM_LIMIT = 40 * 1024 * 1024
PACK_VMEM_LIMIT = 53 * 1024 * 1024 + 512 * 1024
LOAD_VMEM_LIMIT = 51 * 1024 * 1024
NUMBER_VMEM_LIMIT = 50 * 1024 * 1024
LOAD_PIECES = 8

WHOLE = pl.BlockSpec(memory_space=pltpu.VMEM)
ANYWHERE = pl.BlockSpec(memory_space=pl.ANY)


def across(a, b):
    return lax.dot_general(a, b, (((1,), (1,)), ((), ())), preferred_element_type=jnp.float32)


def times(a, b):
    return jnp.dot(a, b, preferred_element_type=jnp.float32)


def joined(pieces, axis):
    return pieces[0] if len(pieces) == 1 else jnp.concatenate(pieces, axis=axis)


def pack_kernel(k_ref, v_ref, *refs, first_of):
    *out_refs, sems = refs
    rows = k_ref.shape[0]
    first = first_of(lax.axis_index("kv"))
    copies = []
    for chunk, out_ref in enumerate(out_refs):
        columns = pl.ds(pl.multiple_of((first + chunk) * HEAD_SIZE, HEAD_SIZE), HEAD_SIZE)
        for part, ref in enumerate((k_ref, v_ref)):
            copies.append(
                pltpu.make_async_copy(
                    ref.at[:, columns],
                    out_ref.at[pl.ds(part * rows, rows), :],
                    sems.at[2 * chunk + part],
                )
            )
    for copy in copies:
        copy.start()
    for copy in copies:
        copy.wait()


def number_kernel(seg_ref, own_ref, out_ref):
    rows = seg_ref.shape[1]
    numbers = jnp.broadcast_to(seg_ref[...].astype(jnp.float32) + 1.0, (number_rows(rows), rows))
    pieces = [numbers[:, at : at + HEAD_SIZE] for at in range(0, rows, HEAD_SIZE)]
    tail = joined(pieces, 0).astype(jnp.bfloat16)
    out_ref[: 2 * rows, :] = own_ref[: 2 * rows, :]
    out_ref[pl.ds(2 * rows, tail.shape[0]), :] = tail


def load_kernel(q_ref, g_ref, own_ref, q_out_ref, g_out_ref, sems):
    pieces = sems.shape[1]
    count = q_ref.shape[0] // pieces
    copies = []
    for piece in range(pieces):
        here = slice(piece * count, (piece + 1) * count)
        for part, (ref, out_ref) in enumerate(((q_ref, q_out_ref), (g_ref, g_out_ref))):
            copies.append(
                pltpu.make_async_copy(
                    ref.at[here, :], out_ref.at[here, :], sems.at[part, piece]
                )
            )
    for copy in copies:
        copy.start()
    for copy in copies:
        copy.wait()


def number_rows(rows):
    return max(SEGMENT_ROWS * HEAD_SIZE // rows, 1)


def segment_row(ref, rows):
    repeat = number_rows(rows)
    count = repeat * rows // HEAD_SIZE
    tail = ref[pl.ds(ref.shape[0] - count, count), :].astype(jnp.float32)
    return joined([tail[at : at + 1] for at in range(0, tail.shape[0], repeat)], 1)


def fill_bias(bias_ref, own_ref, kv_ref, step):
    rows = bias_ref.shape[0]
    q_seg = segment_row(own_ref, rows)
    k_seg = segment_row(kv_ref, rows)
    k_col = jnp.broadcast_to(k_seg, (8, rows)).T[:, :1]
    allowed = k_col == q_seg
    if step == 0:
        k_pos = lax.broadcasted_iota(jnp.int32, (rows, rows), 0)
        q_pos = lax.broadcasted_iota(jnp.int32, (rows, rows), 1)
        allowed = allowed & (k_pos <= q_pos)
    bias_ref[...] = jnp.where(allowed, 0.0, FILL_LOW)


def activity(own_ref, kv_ref, step, rows):
    q_seg = segment_row(own_ref, rows)
    k_seg = segment_row(kv_ref, rows)
    reached = lax.axis_index("ctx") >= step
    active = reached & (k_seg[0, rows - 1] >= q_seg[0, 0]) & (k_seg[0, 0] <= q_seg[0, rows - 1])
    return active, k_seg[0, rows // 2 - 1] >= q_seg[0, 0]


def full_units(per_kv, rows):
    return [(slice(0, rows), [(head, slice(0, rows))]) for head in range(per_kv)]


def own_units(per_kv, rows):
    half = rows // 2
    units = []
    for head in range(0, per_kv, 2):
        units += [(slice(0, half), [(head + i, slice(0, rows))]) for i in range(2)]
        units.append((slice(half, rows), [(head + i, slice(half, rows)) for i in range(2)]))
    return units


def late_units(per_kv, rows):
    return [(slice(rows // 2, rows), [(head, slice(0, rows))]) for head in range(per_kv)]


def early_units(per_kv, rows):
    early = slice(0, rows // 2)
    return [(slice(0, rows), [(head, early), (head + 1, early)]) for head in range(0, per_kv, 2)]


class Unit:
    def __init__(self, unit, base, q_ref, g_ref, kv_ref, bias_ref):
        self.keys, self.parts = unit
        self.rows = kv_ref.shape[0] // 2
        self.bias_ref = bias_ref
        rows = bias_ref.shape[0]
        self.q = self.gather(q_ref, base)
        self.g = self.gather(g_ref, base)
        k = kv_ref[self.keys, :]
        v = kv_ref[slice(rows + self.keys.start, rows + self.keys.stop), :]
        self.raw = across(k, self.q)
        self.dprobs = across(v, self.g)

    def gather(self, ref, base):
        return joined(
            [ref[span, (base + head) * HEAD_SIZE : (base + head + 1) * HEAD_SIZE] for head, span in self.parts],
            0,
        )

    def row(self, ref, part):
        return joined([ref[part, head : head + 1, span] for head, span in self.parts], 1)

    def put_row(self, ref, part, value):
        for (head, span), piece in zip(self.parts, self.split(value)):
            ref[part, head : head + 1, span] = piece

    def split(self, value):
        at, pieces = 0, []
        for _, span in self.parts:
            width = span.stop - span.start
            pieces.append(value[:, at : at + width])
            at += width
        return pieces

    def tiles(self):
        for first in range(0, self.keys.stop - self.keys.start, TILE):
            here = slice(first, first + TILE)
            key_rows = slice(self.keys.start + first, self.keys.start + first + TILE)
            bias = joined([self.bias_ref[key_rows, span] for _, span in self.parts], 1)
            yield bias, self.raw[here], self.dprobs[here]

    def updated(self, stats, factor):
        scores, top = [], None
        for bias, raw, _ in self.tiles():
            scores.append(raw * factor + bias)
            top = scores[-1] if top is None else jnp.maximum(top, scores[-1])
        peak = jnp.max(top, axis=0, keepdims=True)
        if stats is not None:
            peak = jnp.maximum(peak, stats[0])
        weights, total, weighted = [], None, None
        for tile, (_, _, dprobs) in zip(scores, self.tiles()):
            weights.append(jnp.exp2(tile - peak))
            product = weights[-1] * dprobs
            total = weights[-1] if total is None else total + weights[-1]
            weighted = product if weighted is None else weighted + product
        total = jnp.sum(total, axis=0, keepdims=True)
        weighted = jnp.sum(weighted, axis=0, keepdims=True)
        if stats is not None:
            fade = jnp.exp2(stats[0] - peak)
            total = total + stats[1] * fade
            weighted = weighted + stats[2] * fade
        return (peak, total, weighted), weights

    def lowered(self, log_total, delta, factor, weights=None, inverse=None):
        probs, dscores = [], []
        for index, (bias, raw, dprobs) in enumerate(self.tiles()):
            if weights is None:
                tile = jnp.exp2(raw * factor + bias - log_total)
            else:
                tile = weights[index] * inverse
            probs.append(tile.astype(jnp.bfloat16))
            dscores.append((tile * (dprobs - delta)).astype(jnp.bfloat16))
        self.probs, self.dscores = joined(probs, 0), joined(dscores, 0)


def in_turn(units, make, handle, count):
    made = [make(unit) for unit in units[:count]]
    for index in range(len(units)):
        if index + count < len(units):
            made.append(make(units[index + count]))
        handle(made[index])
        made[index] = None


class GradSum:
    def __init__(self, acc_ref, rows):
        self.acc_ref, self.rows, self.waiting, self.seen = acc_ref, rows, {}, set()

    def add(self, unit):
        key = unit.keys.start, unit.keys.stop
        self.waiting.setdefault(key, []).append(unit)
        if len(self.waiting[key]) == 2:
            self.flush(key)

    def flush(self, key):
        units = self.waiting.pop(key)
        first, last = key
        for offset, lhs, rhs in (
            (0, joined([u.dscores for u in units], 1), joined([u.q for u in units], 0)),
            (self.rows, joined([u.probs for u in units], 1), joined([u.g for u in units], 0)),
        ):
            here = slice(offset + first, offset + last)
            term = times(lhs, rhs)
            self.acc_ref[here, :] = self.acc_ref[here, :] + term if key in self.seen else term
        self.seen.add(key)

    def finish(self):
        for key in list(self.waiting):
            self.flush(key)


def finals(stats):
    return stats[0] + jnp.log2(stats[1]), stats[2] / stats[1]


def stats_kernel(ins, outs, _, *, fill, chunk, per_kv, factor, step):
    q_ref, g_ref, own_seg_ref, kv_ref, kv_seg_ref = ins[:5]
    in_ref = ins[5] if step else None
    out_ref = outs[0]
    bias_ref = outs[1] if fill else ins[-1]
    rows = q_ref.shape[0]

    def run():
        if fill:
            fill_bias(bias_ref, own_seg_ref, kv_seg_ref, step)

        def handle(unit):
            source = in_ref
            if step == 0:
                source = out_ref if unit.keys.start > 0 else None
            stats = None if source is None else tuple(unit.row(source, part) for part in range(3))
            for part, value in enumerate(unit.updated(stats, factor)[0]):
                unit.put_row(out_ref, part, value)

        units = full_units(per_kv, rows) if step else own_units(per_kv, rows)
        in_turn(units, lambda unit: Unit(unit, chunk * per_kv, q_ref, g_ref, kv_ref, bias_ref), handle, AHEAD)

    if step == 0:
        run()
        return
    active, _ = activity(own_seg_ref, kv_seg_ref, step, rows)
    pl.when(active)(run)

    @pl.when(jnp.logical_not(active))
    def _():
        out_ref[...] = in_ref[...]


def far_kernel(ins, outs, scratch, *, fill, chunk, per_kv, factor, step):
    q_ref, g_ref, own_seg_ref, kv_ref, kv_seg_ref, in_ref = ins[:6]
    out_ref, kv_grad_ref, dq_ref = outs[:3]
    bias_ref = outs[3] if fill else ins[-1]
    kt_ref, acc_ref = scratch
    rows = q_ref.shape[0]
    half = rows // 2
    active, early = activity(own_seg_ref, kv_seg_ref, step, rows)
    log_total, delta = finals((in_ref[0], in_ref[1], in_ref[2]))
    out_ref[0] = log_total
    out_ref[1] = delta

    def run(units, keys):
        if fill:
            fill_bias(bias_ref, own_seg_ref, kv_seg_ref, step)
        kt_ref[...] = kv_ref[:rows, :].T
        if keys.start > 0:
            for offset in (0, rows):
                acc_ref[offset : offset + keys.start, :] = jnp.zeros((keys.start, HEAD_SIZE), jnp.float32)
        grads = GradSum(acc_ref, rows)

        def first(unit):
            stats = tuple(unit.row(in_ref, part) for part in range(3))
            stats, unit.weights = unit.updated(stats, factor)
            unit.finals = finals(stats)
            unit.inverse = 1.0 / stats[1]
            unit.put_row(out_ref, 0, unit.finals[0])
            unit.put_row(out_ref, 1, unit.finals[1])

        def second(unit):
            unit.lowered(*unit.finals, factor, unit.weights, unit.inverse)
            grads.add(unit)
            dq = times(kt_ref[:, unit.keys], unit.dscores)
            for (head, span), piece in zip(unit.parts, unit.split(dq)):
                dq_ref[head, :, span] = piece
                if span.stop < rows:
                    dq_ref[head, :, span.stop :] = jnp.zeros((HEAD_SIZE, rows - span.stop), jnp.float32)

        def both(unit):
            first(unit)
            second(unit)

        def make(unit):
            return Unit(unit, chunk * per_kv, q_ref, g_ref, kv_ref, bias_ref)

        if chunk % 2:
            made = []
            in_turn(units, make, lambda unit: (first(unit), made.append(unit)), AHEAD)
            for unit in made:
                second(unit)
        else:
            in_turn(units, make, both, AHEAD)
        grads.finish()
        kv_grad_ref[...] = acc_ref[...].astype(kv_grad_ref.dtype)

    @pl.when(active & jnp.logical_not(early))
    def _():
        run(late_units(per_kv, rows), slice(half, rows))

    @pl.when(active & early)
    def _():
        run(early_units(per_kv, rows), slice(0, rows))

    @pl.when(jnp.logical_not(active))
    def _():
        dq_ref[...] = jnp.zeros_like(dq_ref)
        kv_grad_ref[...] = jnp.zeros_like(kv_grad_ref)


def grads_kernel(ins, outs, scratch, *, early_own, chunk, per_kv, factor, scale, step):
    q_ref, g_ref, own_seg_ref, kv_ref, kv_seg_ref, in_ref, dq_in_ref, bias_ref = ins[:8]
    kv_grad_ref, dq_ref = outs[:2]
    kt_ref = scratch[0]
    rows = q_ref.shape[0]

    def make(unit):
        return Unit(unit, chunk * per_kv, q_ref, g_ref, kv_ref, bias_ref)

    def run():
        kt_ref[...] = kv_ref[:rows, :].T
        grads = GradSum(kv_grad_ref, rows)

        def handle(unit):
            unit.lowered(unit.row(in_ref, 0), unit.row(in_ref, 1), factor)
            grads.add(unit)
            head = unit.parts[0][0]
            dq_ref[head] = dq_in_ref[head] + times(kt_ref[:, unit.keys], unit.dscores)

        in_turn(full_units(per_kv, rows), make, handle, AHEAD)
        grads.finish()

    active, _ = activity(own_seg_ref, kv_seg_ref, step, rows)
    pl.when(active)(run)

    @pl.when(jnp.logical_not(active))
    def _():
        kv_grad_ref[...] = jnp.zeros_like(kv_grad_ref)
        dq_ref[...] = dq_in_ref[...]
        if early_own:
            own_kv_ref, own_bias_ref = ins[8:]
            own_run(
                (q_ref, g_ref, own_kv_ref, in_ref, dq_in_ref, own_bias_ref), outs[2:], scratch,
                chunk, per_kv, factor, scale,
            )


def own_run(ins, outs, scratch, chunk, per_kv, factor, scale):
    q_ref, g_ref, kv_ref, in_ref, dq_in_ref, bias_ref = ins
    kv_grad_ref, query_grad_ref = outs
    kt_ref, turned_ref, sems = scratch
    rows = q_ref.shape[0]
    half = rows // 2
    kt_ref[...] = kv_ref[:rows, :].T
    grads = GradSum(kv_grad_ref, rows)
    dq_now, copies = {}, []

    def send(head, count):
        here = slice(head * HEAD_SIZE, (head + count) * HEAD_SIZE)
        there = slice((chunk * per_kv + head) * HEAD_SIZE, (chunk * per_kv + head + count) * HEAD_SIZE)
        copies.append(
            pltpu.make_async_copy(turned_ref.at[:, here], query_grad_ref.at[:, there], sems.at[head // count])
        )
        copies[-1].start()

    def handle(unit):
        unit.lowered(unit.row(in_ref, 0), unit.row(in_ref, 1), factor)
        grads.add(unit)
        dq = times(kt_ref[:, unit.keys], unit.dscores)
        head = unit.parts[0][0]
        if unit.keys.start == 0:
            dq_now[head] = dq_in_ref[head] + dq
            return
        for (other, _), piece in zip(unit.parts, unit.split(dq)):
            total = dq_now.pop(other)
            for at, value in ((0, total[:, :half]), (half, total[:, half:] + piece)):
                turned_ref[at : at + half, other * HEAD_SIZE : (other + 1) * HEAD_SIZE] = (
                    (value * scale).astype(jnp.bfloat16).T
                )
        send(head, len(unit.parts))

    def make(unit):
        return Unit(unit, chunk * per_kv, q_ref, g_ref, kv_ref, bias_ref)

    in_turn(own_units(per_kv, rows), make, handle, AHEAD)
    grads.finish()
    for copy in copies:
        copy.wait()


def own_kernel(ins, outs, scratch, *, done_before, chunk, per_kv, factor, scale):
    q_ref, g_ref, own_seg_ref, kv_ref, kv_seg_ref, in_ref, dq_in_ref, bias_ref = ins[:8]

    def run():
        own_run(
            (q_ref, g_ref, kv_ref, in_ref, dq_in_ref, bias_ref), outs, scratch,
            chunk, per_kv, factor, scale,
        )

    if not done_before:
        run()
        return
    active, _ = activity(own_seg_ref, kv_seg_ref, 1, q_ref.shape[0])
    pl.when(active)(run)

    @pl.when(jnp.logical_not(active))
    def _():
        outs[0][...] = ins[8][...]


def finish_kernel(ins, outs, _, *, scale):
    own_ref, arrived_ref = ins
    rows = own_ref.shape[0] // 2
    for first, factor in ((0, scale), (rows, 1.0)):
        here = slice(first, first + rows)
        total = (own_ref[here, :] + arrived_ref[here, :].astype(jnp.float32)) * factor
        outs[0][here, :] = total.astype(jnp.bfloat16)


def place_kernel(mine_ref, other_ref, *refs, chunk, chunks):
    *out_refs, sems = refs[-3:]
    rows = out_refs[0].shape[0]
    core = lax.axis_index("kv")
    copies = []
    for place, ref in enumerate((mine_ref, other_ref)):
        first = ((1 - core if place else core) * chunks + chunk) * HEAD_SIZE
        columns = pl.ds(pl.multiple_of(first, HEAD_SIZE), HEAD_SIZE)
        for part, out_ref in enumerate(out_refs):
            copies.append(
                pltpu.make_async_copy(
                    ref.at[pl.ds(part * rows, rows), :], out_ref.at[:, columns], sems.at[place, part]
                )
            )
    for copy in copies:
        copy.start()
    for copy in copies:
        copy.wait()


def shards(queries, key_matrix, value_matrix, out_grad, segments):
    rows = queries.shape[0]
    heads = queries.shape[1] // HEAD_SIZE
    group_width = QUERY_HEADS // KEY_VALUE_HEADS
    chunks = max(heads // group_width, 1)
    per_kv = heads // chunks
    ctx = lax.axis_size("ctx")
    groups = lax.axis_size("groups")
    longest = rows * ctx // 2
    reach = min(ctx - 1, (longest - 1 + rows - 1) // rows)
    scale = HEAD_SIZE ** (-0.5)
    factor = scale * LOG2_E
    tail = number_rows(rows) * rows // HEAD_SIZE
    block_shapes = tuple(
        jax.ShapeDtypeStruct((2 * rows + (0 if chunk else tail), HEAD_SIZE), jnp.bfloat16)
        for chunk in range(chunks)
    )
    pairs = per_kv * rows * rows
    each = range(chunks)

    def first_of(kv_index):
        return kv_index * heads // group_width

    def up(step):
        route = []
        for group in range(groups):
            at = group * ctx
            beside = (group + 1) % groups * ctx
            route += [(at + i, beside + i) for i in range(step - 1)]
            route += [(at + i, at + i + 1) for i in range(step - 1, ctx - 1)]
            route.append((at + ctx - 1, at + step - 1))
        return route

    down = [
        (group * ctx + (i + 1) % ctx, group * ctx + i) for group in range(groups) for i in range(ctx)
    ]

    def moved(array, route):
        return lax.ppermute(array, ("groups", "ctx"), route)

    def call(body, operands, outs, scratch, name, micros, out_specs=None, into=(), after=()):
        count = len(operands)
        extra = [array for array, _ in into] + list(after)
        specs = [out_specs[index] for _, index in into] + [ANYWHERE] * len(after)

        def kernel(*refs):
            rest = refs[count + len(extra) :]
            body(refs[:count], rest[: len(outs)], rest[len(outs) :])

        return pl.pallas_call(
            kernel,
            out_shape=outs,
            in_specs=[WHOLE] * count + specs,
            out_specs=out_specs or (WHOLE,) * len(outs),
            scratch_shapes=scratch,
            input_output_aliases={count + place: index for place, (_, index) in enumerate(into)},
            compiler_params=pltpu.CompilerParams(vmem_limit_bytes=VMEM_LIMIT),
            cost_estimate=pl.CostEstimate(
                flops=int(1153e6 * micros * HINT), bytes_accessed=4 * pairs // rows, transcendentals=pairs
            ),
            name=name,
        )(*operands, *extra)

    own = pl.pallas_call(
        functools.partial(pack_kernel, first_of=first_of),
        out_shape=block_shapes,
        in_specs=[ANYWHERE] * 2,
        out_specs=(WHOLE,) * chunks,
        scratch_shapes=[pltpu.SemaphoreType.DMA((2 * chunks,))],
        compiler_params=pltpu.CompilerParams(vmem_limit_bytes=PACK_VMEM_LIMIT),
        cost_estimate=pl.CostEstimate(flops=0, bytes_accessed=4 * 1024 * 1024, transcendentals=0),
        name="pack",
    )(key_matrix, value_matrix)
    own = list(own)
    own[0] = pl.pallas_call(
        number_kernel,
        out_shape=block_shapes[0],
        in_specs=[WHOLE] * 2,
        out_specs=WHOLE,
        input_output_aliases={1: 0},
        compiler_params=pltpu.CompilerParams(vmem_limit_bytes=NUMBER_VMEM_LIMIT),
        name="number",
    )(segments.reshape(1, rows), own[0])

    rows_shape = jax.ShapeDtypeStruct(queries.shape, jnp.bfloat16)
    queries, out_grad = pl.pallas_call(
        load_kernel,
        out_shape=(rows_shape, rows_shape),
        in_specs=[ANYWHERE] * 3,
        out_specs=(WHOLE, WHOLE),
        scratch_shapes=[pltpu.SemaphoreType.DMA((2, LOAD_PIECES))],
        compiler_params=pltpu.CompilerParams(vmem_limit_bytes=LOAD_VMEM_LIMIT),
        name="load",
    )(queries, out_grad, own[0])

    turned = pltpu.VMEM((HEAD_SIZE, rows), jnp.bfloat16)
    total_sum = pltpu.VMEM((2 * rows, HEAD_SIZE), jnp.float32)
    bias_shape = jax.ShapeDtypeStruct((rows, rows), jnp.float32)
    stats_shape = jax.ShapeDtypeStruct((3, per_kv, rows), jnp.float32)
    finals_shape = jax.ShapeDtypeStruct((2, per_kv, rows), jnp.float32)
    dq_shape = jax.ShapeDtypeStruct((per_kv, HEAD_SIZE, rows), jnp.float32)
    kv_grad_shape = jax.ShapeDtypeStruct((2 * rows, HEAD_SIZE), jnp.float32)
    sent_shape = jax.ShapeDtypeStruct((2 * rows, HEAD_SIZE), jnp.bfloat16)
    common = {"per_kv": per_kv, "factor": factor}
    biases = [None] * (reach + 1)
    own = list(lax.optimization_barrier(tuple(own)))
    blocks = [[own[chunk], moved(own[chunk], up(1))] for chunk in each]

    def common_operands(chunk, step):
        return queries, out_grad, own[0], blocks[chunk][step], blocks[0][step]

    def with_bias(kernel, chunk, step, operands, outs, scratch, name, micros, after=()):
        fill = biases[step] is None
        body = functools.partial(kernel, fill=fill, chunk=chunk, step=step, **common)
        operands = common_operands(chunk, step) + operands
        if not fill:
            return call(body, operands + (biases[step],), outs, scratch, name, micros, after=after)
        *results, biases[step] = call(
            body, operands, outs + (bias_shape,), scratch, name, micros, after=after
        )
        return results

    stats, final_stats = [None] * chunks, [None] * chunks
    sums, dq = [None] * chunks, [None] * chunks
    for chunk in each:
        after = [blocks[chunk - 1][1]] if chunk else []
        (stats[chunk],) = with_bias(
            stats_kernel, chunk, 0, (), (stats_shape,), [], "stats_own", 0.8, after
        )
    for step in range(1, reach):
        for chunk in each:
            here, stats[chunk] = lax.optimization_barrier((blocks[chunk][step], stats[chunk]))
            blocks[chunk].append(moved(here, up(step + 1)))
        for chunk in each:
            (stats[chunk],) = with_bias(
                stats_kernel, chunk, step, (stats[chunk],), (stats_shape,), [], "stats", 1.1
            )
    before = [stats[-1]]
    for chunk in each:
        final_stats[chunk], sums[chunk], dq[chunk] = with_bias(
            far_kernel, chunk, reach, (stats[chunk],), (finals_shape, sent_shape, dq_shape),
            [turned, total_sum], "grads_far", 1.6, before,
        )
        before = [sums[chunk]]
    finished, returning, query_grad = [None] * chunks, [], []
    own_outs = (kv_grad_shape, jax.ShapeDtypeStruct(queries.shape, jnp.bfloat16))
    own_specs = (WHOLE, ANYWHERE)
    own_scratch = [
        turned,
        pltpu.VMEM((rows, per_kv * HEAD_SIZE), jnp.bfloat16),
        pltpu.SemaphoreType.DMA((per_kv // 2,)),
    ]

    def own_grads(chunk):
        done_before = finished[chunk] is not None
        body = functools.partial(own_kernel, done_before=done_before, chunk=chunk, scale=scale, **common)
        into = [(query_grad.pop(), 1)] if query_grad else []
        seen = 1 if done_before else 0
        finished[chunk], written = call(
            body,
            (queries, out_grad, own[0], blocks[chunk][0], blocks[0][seen])
            + (final_stats[chunk], dq[chunk], biases[0])
            + ((finished[chunk],) if done_before else ()),
            own_outs,
            own_scratch,
            "grads_own",
            1.8,
            out_specs=own_specs,
            into=into,
            after=[sums[chunk]],
        )
        query_grad.append(written)

    for step in range(reach - 1, 0, -1):
        mine = [None] * chunks
        arriving = [moved(sums[chunk], down) for chunk in each]
        for chunk in each:
            early_own = step == 1 and chunk == 0
            body = functools.partial(
                grads_kernel, early_own=early_own, chunk=chunk, step=step, scale=scale, **common
            )
            operands = common_operands(chunk, step) + (final_stats[chunk], dq[chunk], biases[step])
            outs, specs, scratch = (kv_grad_shape, dq_shape), (WHOLE, WHOLE), [turned]
            if early_own:
                operands += (blocks[chunk][0], biases[0])
                outs, specs, scratch = outs + own_outs, specs + own_specs, own_scratch
            mine[chunk], dq[chunk], *rest = call(
                body, operands, outs, scratch, "grads", 1.6, out_specs=specs, after=before
            )
            if early_own:
                finished[chunk] = rest[0]
                query_grad.append(rest[1])
            before = [mine[chunk]]
        arriving[0], mine[-1] = lax.optimization_barrier((arriving[0], mine[-1]))
        for chunk in each:
            here = arriving[chunk]
            if step == 1 and chunk:
                own_grads(chunk - 1)
                here, finished[chunk - 1] = lax.optimization_barrier((here, finished[chunk - 1]))
            sums[chunk] = (mine[chunk] + here.astype(jnp.float32)).astype(jnp.bfloat16)
            if step == 1:
                returning.append(moved(sums[chunk], down))
    if reach == 1:
        returning += [moved(sums[chunk], down) for chunk in each]
    for chunk in each if reach == 1 else each[-1:]:
        own_grads(chunk)

    returning[0], finished[-1] = lax.optimization_barrier((returning[0], finished[-1]))
    kv_swap = [(0, 1), (1, 0)]
    if chunks * lax.axis_size("kv") * HEAD_SIZE > key_matrix.shape[1]:
        key_scale = jnp.where(jnp.arange(2 * rows)[:, None] < rows, scale, 1.0).astype(jnp.float32)
        both = []
        for chunk in each:
            mine = (finished[chunk] + returning[chunk].astype(jnp.float32)).astype(jnp.bfloat16)
            other = lax.ppermute(mine, "kv", kv_swap).astype(jnp.float32)
            both.append(((mine.astype(jnp.float32) + other) * key_scale).astype(jnp.bfloat16))
        both = joined(both, 1)
        return query_grad[0], both[:rows], both[rows:]
    kv_grads, before = (), []
    for chunk in each:
        mine = call(
            functools.partial(finish_kernel, scale=scale),
            (finished[chunk], returning[chunk]),
            (sent_shape,),
            [],
            "finish",
            0.1,
            after=before,
        )[0]
        before = [mine]
        other = lax.ppermute(mine, "kv", kv_swap)
        kv_grads = pl.pallas_call(
            functools.partial(place_kernel, chunk=chunk, chunks=chunks),
            out_shape=(jax.ShapeDtypeStruct(key_matrix.shape, jnp.bfloat16),) * 2,
            in_specs=[WHOLE] * 2 + [ANYWHERE] * len(kv_grads),
            out_specs=(ANYWHERE,) * 2,
            scratch_shapes=[pltpu.SemaphoreType.DMA((2, 2))],
            input_output_aliases={2 + index: index for index in range(len(kv_grads))},
            compiler_params=pltpu.CompilerParams(vmem_limit_bytes=VMEM_LIMIT),
            name="place",
        )(mine, other, *kv_grads)
    return (query_grad[0], *kv_grads)


def solution(mesh):
    return jax.shard_map(
        shards,
        mesh=mesh,
        in_specs=(
            P(("groups", "ctx"), ("tp", "kv")),
            P(("groups", "ctx"), "tp"),
            P(("groups", "ctx"), "tp"),
            P(("groups", "ctx"), ("tp", "kv")),
            P(("groups", "ctx")),
        ),
        out_specs=(
            P(("groups", "ctx"), ("tp", "kv")),
            P(("groups", "ctx"), "tp"),
            P(("groups", "ctx"), "tp"),
        ),
        check_vma=False,
    )
```

```python
import functools
import jax
import jax.numpy as jnp
from jax import lax
from jax.experimental import pallas as pl
from jax.experimental.pallas import tpu as pltpu
from jax.sharding import PartitionSpec as P

QUERY_HEADS = 64
KEY_VALUE_HEADS = 8
HEAD_SIZE = 128
SEGMENT_ROWS = 16
TILE = 32
HINT = 0.2
AHEAD = 3
FILL_LOW = -1e30
LOG2_E = 1.4426950408889634
VMEM_LIMIT = 40 * 1024 * 1024
PACK_VMEM_LIMIT = 53 * 1024 * 1024 + 512 * 1024
LOAD_VMEM_LIMIT = 51 * 1024 * 1024
NUMBER_VMEM_LIMIT = 50 * 1024 * 1024
LOAD_PIECES = 8

WHOLE = pl.BlockSpec(memory_space=pltpu.VMEM)
ANYWHERE = pl.BlockSpec(memory_space=pl.ANY)


def across(a, b):
    return lax.dot_general(a, b, (((1,), (1,)), ((), ())), preferred_element_type=jnp.float32)


def times(a, b):
    return jnp.dot(a, b, preferred_element_type=jnp.float32)


def joined(pieces, axis):
    return pieces[0] if len(pieces) == 1 else jnp.concatenate(pieces, axis=axis)


def pack_kernel(k_ref, v_ref, *refs, first_of):
    *out_refs, sems = refs
    rows = k_ref.shape[0]
    first = first_of(lax.axis_index("kv"))
    copies = []
    for chunk, out_ref in enumerate(out_refs):
        columns = pl.ds(pl.multiple_of((first + chunk) * HEAD_SIZE, HEAD_SIZE), HEAD_SIZE)
        for part, ref in enumerate((k_ref, v_ref)):
            copies.append(
                pltpu.make_async_copy(
                    ref.at[:, columns],
                    out_ref.at[pl.ds(part * rows, rows), :],
                    sems.at[2 * chunk + part],
                )
            )
    for copy in copies:
        copy.start()
    for copy in copies:
        copy.wait()


def number_kernel(seg_ref, own_ref, out_ref):
    rows = seg_ref.shape[1]
    numbers = jnp.broadcast_to(seg_ref[...].astype(jnp.float32) + 1.0, (number_rows(rows), rows))
    pieces = [numbers[:, at : at + HEAD_SIZE] for at in range(0, rows, HEAD_SIZE)]
    tail = joined(pieces, 0).astype(jnp.bfloat16)
    out_ref[: 2 * rows, :] = own_ref[: 2 * rows, :]
    out_ref[pl.ds(2 * rows, tail.shape[0]), :] = tail


def load_kernel(q_ref, g_ref, own_ref, q_out_ref, g_out_ref, sems):
    pieces = sems.shape[1]
    count = q_ref.shape[0] // pieces
    copies = []
    for piece in range(pieces):
        here = slice(piece * count, (piece + 1) * count)
        for part, (ref, out_ref) in enumerate(((q_ref, q_out_ref), (g_ref, g_out_ref))):
            copies.append(
                pltpu.make_async_copy(
                    ref.at[here, :], out_ref.at[here, :], sems.at[part, piece]
                )
            )
    for copy in copies:
        copy.start()
    for copy in copies:
        copy.wait()


def number_rows(rows):
    return max(SEGMENT_ROWS * HEAD_SIZE // rows, 1)


def segment_row(ref, rows):
    repeat = number_rows(rows)
    count = repeat * rows // HEAD_SIZE
    tail = ref[pl.ds(ref.shape[0] - count, count), :].astype(jnp.float32)
    return joined([tail[at : at + 1] for at in range(0, tail.shape[0], repeat)], 1)


def fill_bias(bias_ref, own_ref, kv_ref, step):
    rows = bias_ref.shape[0]
    q_seg = segment_row(own_ref, rows)
    k_seg = segment_row(kv_ref, rows)
    k_col = jnp.broadcast_to(k_seg, (8, rows)).T[:, :1]
    allowed = k_col == q_seg
    if step == 0:
        k_pos = lax.broadcasted_iota(jnp.int32, (rows, rows), 0)
        q_pos = lax.broadcasted_iota(jnp.int32, (rows, rows), 1)
        allowed = allowed & (k_pos <= q_pos)
    bias_ref[...] = jnp.where(allowed, 0.0, FILL_LOW)


def activity(own_ref, kv_ref, step, rows):
    q_seg = segment_row(own_ref, rows)
    k_seg = segment_row(kv_ref, rows)
    reached = lax.axis_index("ctx") >= step
    active = reached & (k_seg[0, rows - 1] >= q_seg[0, 0]) & (k_seg[0, 0] <= q_seg[0, rows - 1])
    return active, k_seg[0, rows // 2 - 1] >= q_seg[0, 0]


def full_units(per_kv, rows):
    return [(slice(0, rows), [(head, slice(0, rows))]) for head in range(per_kv)]


def own_units(per_kv, rows):
    half = rows // 2
    units = []
    for head in range(0, per_kv, 2):
        units += [(slice(0, half), [(head + i, slice(0, rows))]) for i in range(2)]
        units.append((slice(half, rows), [(head + i, slice(half, rows)) for i in range(2)]))
    return units


def late_units(per_kv, rows):
    return [(slice(rows // 2, rows), [(head, slice(0, rows))]) for head in range(per_kv)]


def early_units(per_kv, rows):
    early = slice(0, rows // 2)
    return [(slice(0, rows), [(head, early), (head + 1, early)]) for head in range(0, per_kv, 2)]


class Unit:
    def __init__(self, unit, base, q_ref, g_ref, kv_ref, bias_ref):
        self.keys, self.parts = unit
        self.rows = kv_ref.shape[0] // 2
        self.bias_ref = bias_ref
        rows = bias_ref.shape[0]
        self.q = self.gather(q_ref, base)
        self.g = self.gather(g_ref, base)
        k = kv_ref[self.keys, :]
        v = kv_ref[slice(rows + self.keys.start, rows + self.keys.stop), :]
        self.raw = across(k, self.q)
        self.dprobs = across(v, self.g)

    def gather(self, ref, base):
        return joined(
            [ref[span, (base + head) * HEAD_SIZE : (base + head + 1) * HEAD_SIZE] for head, span in self.parts],
            0,
        )

    def row(self, ref, part):
        return joined([ref[part, head : head + 1, span] for head, span in self.parts], 1)

    def put_row(self, ref, part, value):
        for (head, span), piece in zip(self.parts, self.split(value)):
            ref[part, head : head + 1, span] = piece

    def split(self, value):
        at, pieces = 0, []
        for _, span in self.parts:
            width = span.stop - span.start
            pieces.append(value[:, at : at + width])
            at += width
        return pieces

    def tiles(self):
        for first in range(0, self.keys.stop - self.keys.start, TILE):
            here = slice(first, first + TILE)
            key_rows = slice(self.keys.start + first, self.keys.start + first + TILE)
            bias = joined([self.bias_ref[key_rows, span] for _, span in self.parts], 1)
            yield bias, self.raw[here], self.dprobs[here]

    def updated(self, stats, factor):
        scores, top = [], None
        for bias, raw, _ in self.tiles():
            scores.append(raw * factor + bias)
            top = scores[-1] if top is None else jnp.maximum(top, scores[-1])
        peak = jnp.max(top, axis=0, keepdims=True)
        if stats is not None:
            peak = jnp.maximum(peak, stats[0])
        weights, total, weighted = [], None, None
        for tile, (_, _, dprobs) in zip(scores, self.tiles()):
            weights.append(jnp.exp2(tile - peak))
            product = weights[-1] * dprobs
            total = weights[-1] if total is None else total + weights[-1]
            weighted = product if weighted is None else weighted + product
        total = jnp.sum(total, axis=0, keepdims=True)
        weighted = jnp.sum(weighted, axis=0, keepdims=True)
        if stats is not None:
            fade = jnp.exp2(stats[0] - peak)
            total = total + stats[1] * fade
            weighted = weighted + stats[2] * fade
        return (peak, total, weighted), weights

    def lowered(self, log_total, delta, factor, weights=None, inverse=None):
        probs, dscores = [], []
        for index, (bias, raw, dprobs) in enumerate(self.tiles()):
            if weights is None:
                tile = jnp.exp2(raw * factor + bias - log_total)
            else:
                tile = weights[index] * inverse
            probs.append(tile.astype(jnp.bfloat16))
            dscores.append((tile * (dprobs - delta)).astype(jnp.bfloat16))
        self.probs, self.dscores = joined(probs, 0), joined(dscores, 0)


def in_turn(units, make, handle, count):
    made = [make(unit) for unit in units[:count]]
    for index in range(len(units)):
        if index + count < len(units):
            made.append(make(units[index + count]))
        handle(made[index])
        made[index] = None


class GradSum:
    def __init__(self, acc_ref, rows):
        self.acc_ref, self.rows, self.waiting, self.seen = acc_ref, rows, {}, set()

    def add(self, unit):
        key = unit.keys.start, unit.keys.stop
        self.waiting.setdefault(key, []).append(unit)
        if len(self.waiting[key]) == 2:
            self.flush(key)

    def flush(self, key):
        units = self.waiting.pop(key)
        first, last = key
        for offset, lhs, rhs in (
            (0, joined([u.dscores for u in units], 1), joined([u.q for u in units], 0)),
            (self.rows, joined([u.probs for u in units], 1), joined([u.g for u in units], 0)),
        ):
            here = slice(offset + first, offset + last)
            term = times(lhs, rhs)
            self.acc_ref[here, :] = self.acc_ref[here, :] + term if key in self.seen else term
        self.seen.add(key)

    def finish(self):
        for key in list(self.waiting):
            self.flush(key)


def finals(stats):
    return stats[0] + jnp.log2(stats[1]), stats[2] / stats[1]


def stats_kernel(ins, outs, _, *, fill, chunk, per_kv, factor, step):
    q_ref, g_ref, own_seg_ref, kv_ref, kv_seg_ref = ins[:5]
    in_ref = ins[5] if step else None
    out_ref = outs[0]
    bias_ref = outs[1] if fill else ins[-1]
    rows = q_ref.shape[0]

    def run():
        if fill:
            fill_bias(bias_ref, own_seg_ref, kv_seg_ref, step)

        def handle(unit):
            source = in_ref
            if step == 0:
                source = out_ref if unit.keys.start > 0 else None
            stats = None if source is None else tuple(unit.row(source, part) for part in range(3))
            for part, value in enumerate(unit.updated(stats, factor)[0]):
                unit.put_row(out_ref, part, value)

        units = full_units(per_kv, rows) if step else own_units(per_kv, rows)
        in_turn(units, lambda unit: Unit(unit, chunk * per_kv, q_ref, g_ref, kv_ref, bias_ref), handle, AHEAD)

    if step == 0:
        run()
        return
    active, _ = activity(own_seg_ref, kv_seg_ref, step, rows)
    pl.when(active)(run)

    @pl.when(jnp.logical_not(active))
    def _():
        out_ref[...] = in_ref[...]


def far_kernel(ins, outs, scratch, *, fill, chunk, per_kv, factor, step):
    q_ref, g_ref, own_seg_ref, kv_ref, kv_seg_ref, in_ref = ins[:6]
    out_ref, kv_grad_ref, dq_ref = outs[:3]
    bias_ref = outs[3] if fill else ins[-1]
    kt_ref, acc_ref = scratch
    rows = q_ref.shape[0]
    half = rows // 2
    active, early = activity(own_seg_ref, kv_seg_ref, step, rows)
    log_total, delta = finals((in_ref[0], in_ref[1], in_ref[2]))
    out_ref[0] = log_total
    out_ref[1] = delta

    def run(units, keys):
        if fill:
            fill_bias(bias_ref, own_seg_ref, kv_seg_ref, step)
        kt_ref[...] = kv_ref[:rows, :].T
        if keys.start > 0:
            for offset in (0, rows):
                acc_ref[offset : offset + keys.start, :] = jnp.zeros((keys.start, HEAD_SIZE), jnp.float32)
        grads = GradSum(acc_ref, rows)

        def first(unit):
            stats = tuple(unit.row(in_ref, part) for part in range(3))
            stats, unit.weights = unit.updated(stats, factor)
            unit.finals = finals(stats)
            unit.inverse = 1.0 / stats[1]
            unit.put_row(out_ref, 0, unit.finals[0])
            unit.put_row(out_ref, 1, unit.finals[1])

        def second(unit):
            unit.lowered(*unit.finals, factor, unit.weights, unit.inverse)
            grads.add(unit)
            dq = times(kt_ref[:, unit.keys], unit.dscores)
            for (head, span), piece in zip(unit.parts, unit.split(dq)):
                dq_ref[head, :, span] = piece
                if span.stop < rows:
                    dq_ref[head, :, span.stop :] = jnp.zeros((HEAD_SIZE, rows - span.stop), jnp.float32)

        def both(unit):
            first(unit)
            second(unit)

        def make(unit):
            return Unit(unit, chunk * per_kv, q_ref, g_ref, kv_ref, bias_ref)

        if chunk % 2:
            made = []
            in_turn(units, make, lambda unit: (first(unit), made.append(unit)), AHEAD)
            for unit in made:
                second(unit)
        else:
            in_turn(units, make, both, AHEAD)
        grads.finish()
        kv_grad_ref[...] = acc_ref[...].astype(kv_grad_ref.dtype)

    @pl.when(active & jnp.logical_not(early))
    def _():
        run(late_units(per_kv, rows), slice(half, rows))

    @pl.when(active & early)
    def _():
        run(early_units(per_kv, rows), slice(0, rows))

    @pl.when(jnp.logical_not(active))
    def _():
        dq_ref[...] = jnp.zeros_like(dq_ref)
        kv_grad_ref[...] = jnp.zeros_like(kv_grad_ref)


def grads_kernel(ins, outs, scratch, *, early_own, chunk, per_kv, factor, scale, step):
    q_ref, g_ref, own_seg_ref, kv_ref, kv_seg_ref, in_ref, dq_in_ref, bias_ref = ins[:8]
    kv_grad_ref, dq_ref = outs[:2]
    kt_ref = scratch[0]
    rows = q_ref.shape[0]

    def make(unit):
        return Unit(unit, chunk * per_kv, q_ref, g_ref, kv_ref, bias_ref)

    def run():
        kt_ref[...] = kv_ref[:rows, :].T
        grads = GradSum(kv_grad_ref, rows)

        def handle(unit):
            unit.lowered(unit.row(in_ref, 0), unit.row(in_ref, 1), factor)
            grads.add(unit)
            head = unit.parts[0][0]
            dq_ref[head] = dq_in_ref[head] + times(kt_ref[:, unit.keys], unit.dscores)

        in_turn(full_units(per_kv, rows), make, handle, AHEAD)
        grads.finish()

    active, _ = activity(own_seg_ref, kv_seg_ref, step, rows)
    pl.when(active)(run)

    @pl.when(jnp.logical_not(active))
    def _():
        kv_grad_ref[...] = jnp.zeros_like(kv_grad_ref)
        dq_ref[...] = dq_in_ref[...]
        if early_own:
            own_kv_ref, own_bias_ref = ins[8:]
            own_run(
                (q_ref, g_ref, own_kv_ref, in_ref, dq_in_ref, own_bias_ref), outs[2:], scratch,
                chunk, per_kv, factor, scale,
            )


def own_run(ins, outs, scratch, chunk, per_kv, factor, scale):
    q_ref, g_ref, kv_ref, in_ref, dq_in_ref, bias_ref = ins
    kv_grad_ref, query_grad_ref = outs
    kt_ref, turned_ref, sems = scratch
    rows = q_ref.shape[0]
    half = rows // 2
    kt_ref[...] = kv_ref[:rows, :].T
    grads = GradSum(kv_grad_ref, rows)
    dq_now, copies = {}, []

    def send(head, count):
        here = slice(head * HEAD_SIZE, (head + count) * HEAD_SIZE)
        there = slice((chunk * per_kv + head) * HEAD_SIZE, (chunk * per_kv + head + count) * HEAD_SIZE)
        copies.append(
            pltpu.make_async_copy(turned_ref.at[:, here], query_grad_ref.at[:, there], sems.at[head // count])
        )
        copies[-1].start()

    def handle(unit):
        unit.lowered(unit.row(in_ref, 0), unit.row(in_ref, 1), factor)
        grads.add(unit)
        dq = times(kt_ref[:, unit.keys], unit.dscores)
        head = unit.parts[0][0]
        if unit.keys.start == 0:
            dq_now[head] = dq_in_ref[head] + dq
            return
        for (other, _), piece in zip(unit.parts, unit.split(dq)):
            total = dq_now.pop(other)
            for at, value in ((0, total[:, :half]), (half, total[:, half:] + piece)):
                turned_ref[at : at + half, other * HEAD_SIZE : (other + 1) * HEAD_SIZE] = (
                    (value * scale).astype(jnp.bfloat16).T
                )
        send(head, len(unit.parts))

    def make(unit):
        return Unit(unit, chunk * per_kv, q_ref, g_ref, kv_ref, bias_ref)

    in_turn(own_units(per_kv, rows), make, handle, AHEAD)
    grads.finish()
    for copy in copies:
        copy.wait()


def own_kernel(ins, outs, scratch, *, done_before, chunk, per_kv, factor, scale):
    q_ref, g_ref, own_seg_ref, kv_ref, kv_seg_ref, in_ref, dq_in_ref, bias_ref = ins[:8]

    def run():
        own_run(
            (q_ref, g_ref, kv_ref, in_ref, dq_in_ref, bias_ref), outs, scratch,
            chunk, per_kv, factor, scale,
        )

    if not done_before:
        run()
        return
    active, _ = activity(own_seg_ref, kv_seg_ref, 1, q_ref.shape[0])
    pl.when(active)(run)

    @pl.when(jnp.logical_not(active))
    def _():
        outs[0][...] = ins[8][...]


def finish_kernel(ins, outs, _, *, scale):
    own_ref, arrived_ref = ins
    rows = own_ref.shape[0] // 2
    for first, factor in ((0, scale), (rows, 1.0)):
        here = slice(first, first + rows)
        total = (own_ref[here, :] + arrived_ref[here, :].astype(jnp.float32)) * factor
        outs[0][here, :] = total.astype(jnp.bfloat16)


def place_kernel(mine_ref, other_ref, *refs, chunk, chunks):
    *out_refs, sems = refs[-3:]
    rows = out_refs[0].shape[0]
    core = lax.axis_index("kv")
    copies = []
    for place, ref in enumerate((mine_ref, other_ref)):
        first = ((1 - core if place else core) * chunks + chunk) * HEAD_SIZE
        columns = pl.ds(pl.multiple_of(first, HEAD_SIZE), HEAD_SIZE)
        for part, out_ref in enumerate(out_refs):
            copies.append(
                pltpu.make_async_copy(
                    ref.at[pl.ds(part * rows, rows), :], out_ref.at[:, columns], sems.at[place, part]
                )
            )
    for copy in copies:
        copy.start()
    for copy in copies:
        copy.wait()


def shards(queries, key_matrix, value_matrix, out_grad, segments):
    rows = queries.shape[0]
    heads = queries.shape[1] // HEAD_SIZE
    group_width = QUERY_HEADS // KEY_VALUE_HEADS
    chunks = max(heads // group_width, 1)
    per_kv = heads // chunks
    ctx = lax.axis_size("ctx")
    groups = lax.axis_size("groups")
    longest = rows * ctx // 2
    reach = min(ctx - 1, (longest - 1 + rows - 1) // rows)
    scale = HEAD_SIZE ** (-0.5)
    factor = scale * LOG2_E
    tail = number_rows(rows) * rows // HEAD_SIZE
    block_shapes = tuple(
        jax.ShapeDtypeStruct((2 * rows + (0 if chunk else tail), HEAD_SIZE), jnp.bfloat16)
        for chunk in range(chunks)
    )
    pairs = per_kv * rows * rows
    each = range(chunks)

    def first_of(kv_index):
        return kv_index * heads // group_width

    def up(step):
        route = []
        for group in range(groups):
            at = group * ctx
            beside = (group + 1) % groups * ctx
            route += [(at + i, beside + i) for i in range(step - 1)]
            route += [(at + i, at + i + 1) for i in range(step - 1, ctx - 1)]
            route.append((at + ctx - 1, at + step - 1))
        return route

    def down(step):
        return [(target, source) for source, target in up(step)]

    def moved(array, route):
        return lax.ppermute(array, ("groups", "ctx"), route)

    def call(body, operands, outs, scratch, name, micros, out_specs=None, into=(), after=()):
        count = len(operands)
        extra = [array for array, _ in into] + list(after)
        specs = [out_specs[index] for _, index in into] + [ANYWHERE] * len(after)

        def kernel(*refs):
            rest = refs[count + len(extra) :]
            body(refs[:count], rest[: len(outs)], rest[len(outs) :])

        return pl.pallas_call(
            kernel,
            out_shape=outs,
            in_specs=[WHOLE] * count + specs,
            out_specs=out_specs or (WHOLE,) * len(outs),
            scratch_shapes=scratch,
            input_output_aliases={count + place: index for place, (_, index) in enumerate(into)},
            compiler_params=pltpu.CompilerParams(vmem_limit_bytes=VMEM_LIMIT),
            cost_estimate=pl.CostEstimate(
                flops=int(1153e6 * micros * HINT), bytes_accessed=4 * pairs // rows, transcendentals=pairs
            ),
            name=name,
        )(*operands, *extra)

    own = pl.pallas_call(
        functools.partial(pack_kernel, first_of=first_of),
        out_shape=block_shapes,
        in_specs=[ANYWHERE] * 2,
        out_specs=(WHOLE,) * chunks,
        scratch_shapes=[pltpu.SemaphoreType.DMA((2 * chunks,))],
        compiler_params=pltpu.CompilerParams(vmem_limit_bytes=PACK_VMEM_LIMIT),
        cost_estimate=pl.CostEstimate(flops=0, bytes_accessed=4 * 1024 * 1024, transcendentals=0),
        name="pack",
    )(key_matrix, value_matrix)
    own = list(own)
    own[0] = pl.pallas_call(
        number_kernel,
        out_shape=block_shapes[0],
        in_specs=[WHOLE] * 2,
        out_specs=WHOLE,
        input_output_aliases={1: 0},
        compiler_params=pltpu.CompilerParams(vmem_limit_bytes=NUMBER_VMEM_LIMIT),
        name="number",
    )(segments.reshape(1, rows), own[0])

    rows_shape = jax.ShapeDtypeStruct(queries.shape, jnp.bfloat16)
    queries, out_grad = pl.pallas_call(
        load_kernel,
        out_shape=(rows_shape, rows_shape),
        in_specs=[ANYWHERE] * 3,
        out_specs=(WHOLE, WHOLE),
        scratch_shapes=[pltpu.SemaphoreType.DMA((2, LOAD_PIECES))],
        compiler_params=pltpu.CompilerParams(vmem_limit_bytes=LOAD_VMEM_LIMIT),
        name="load",
    )(queries, out_grad, own[0])

    turned = pltpu.VMEM((HEAD_SIZE, rows), jnp.bfloat16)
    total_sum = pltpu.VMEM((2 * rows, HEAD_SIZE), jnp.float32)
    bias_shape = jax.ShapeDtypeStruct((rows, rows), jnp.float32)
    stats_shape = jax.ShapeDtypeStruct((3, per_kv, rows), jnp.float32)
    finals_shape = jax.ShapeDtypeStruct((2, per_kv, rows), jnp.float32)
    dq_shape = jax.ShapeDtypeStruct((per_kv, HEAD_SIZE, rows), jnp.float32)
    kv_grad_shape = jax.ShapeDtypeStruct((2 * rows, HEAD_SIZE), jnp.float32)
    sent_shape = jax.ShapeDtypeStruct((2 * rows, HEAD_SIZE), jnp.bfloat16)
    common = {"per_kv": per_kv, "factor": factor}
    biases = [None] * (reach + 1)
    own = list(lax.optimization_barrier(tuple(own)))
    blocks = [[own[chunk], moved(own[chunk], up(1))] for chunk in each]

    def common_operands(chunk, step):
        return queries, out_grad, own[0], blocks[chunk][step], blocks[0][step]

    def with_bias(kernel, chunk, step, operands, outs, scratch, name, micros, after=()):
        fill = biases[step] is None
        body = functools.partial(kernel, fill=fill, chunk=chunk, step=step, **common)
        operands = common_operands(chunk, step) + operands
        if not fill:
            return call(body, operands + (biases[step],), outs, scratch, name, micros, after=after)
        *results, biases[step] = call(
            body, operands, outs + (bias_shape,), scratch, name, micros, after=after
        )
        return results

    stats, final_stats = [None] * chunks, [None] * chunks
    sums, dq = [None] * chunks, [None] * chunks
    for chunk in each:
        after = [blocks[chunk - 1][1]] if chunk else []
        (stats[chunk],) = with_bias(
            stats_kernel, chunk, 0, (), (stats_shape,), [], "stats_own", 0.8, after
        )
    for step in range(1, reach):
        for chunk in each:
            here, stats[chunk] = lax.optimization_barrier((blocks[chunk][step], stats[chunk]))
            blocks[chunk].append(moved(here, up(step + 1)))
        for chunk in each:
            (stats[chunk],) = with_bias(
                stats_kernel, chunk, step, (stats[chunk],), (stats_shape,), [], "stats", 1.1
            )
    before = [stats[-1]]
    for chunk in each:
        final_stats[chunk], sums[chunk], dq[chunk] = with_bias(
            far_kernel, chunk, reach, (stats[chunk],), (finals_shape, sent_shape, dq_shape),
            [turned, total_sum], "grads_far", 1.6, before,
        )
        before = [sums[chunk]]
    finished, returning, query_grad = [None] * chunks, [], []
    own_outs = (kv_grad_shape, jax.ShapeDtypeStruct(queries.shape, jnp.bfloat16))
    own_specs = (WHOLE, ANYWHERE)
    own_scratch = [
        turned,
        pltpu.VMEM((rows, per_kv * HEAD_SIZE), jnp.bfloat16),
        pltpu.SemaphoreType.DMA((per_kv // 2,)),
    ]

    def own_grads(chunk):
        done_before = finished[chunk] is not None
        body = functools.partial(own_kernel, done_before=done_before, chunk=chunk, scale=scale, **common)
        into = [(query_grad.pop(), 1)] if query_grad else []
        seen = 1 if done_before else 0
        finished[chunk], written = call(
            body,
            (queries, out_grad, own[0], blocks[chunk][0], blocks[0][seen])
            + (final_stats[chunk], dq[chunk], biases[0])
            + ((finished[chunk],) if done_before else ()),
            own_outs,
            own_scratch,
            "grads_own",
            1.8,
            out_specs=own_specs,
            into=into,
            after=[sums[chunk]],
        )
        query_grad.append(written)

    for step in range(reach - 1, 0, -1):
        mine = [None] * chunks
        arriving = [moved(sums[chunk], down(step + 1)) for chunk in each]
        for chunk in each:
            early_own = step == 1 and chunk == 0
            body = functools.partial(
                grads_kernel, early_own=early_own, chunk=chunk, step=step, scale=scale, **common
            )
            operands = common_operands(chunk, step) + (final_stats[chunk], dq[chunk], biases[step])
            outs, specs, scratch = (kv_grad_shape, dq_shape), (WHOLE, WHOLE), [turned]
            if early_own:
                operands += (blocks[chunk][0], biases[0])
                outs, specs, scratch = outs + own_outs, specs + own_specs, own_scratch
            mine[chunk], dq[chunk], *rest = call(
                body, operands, outs, scratch, "grads", 1.6, out_specs=specs, after=before
            )
            if early_own:
                finished[chunk] = rest[0]
                query_grad.append(rest[1])
            before = [mine[chunk]]
        arriving[0], mine[-1] = lax.optimization_barrier((arriving[0], mine[-1]))
        for chunk in each:
            here = arriving[chunk]
            if step == 1 and chunk:
                own_grads(chunk - 1)
                here, finished[chunk - 1] = lax.optimization_barrier((here, finished[chunk - 1]))
            sums[chunk] = (mine[chunk] + here.astype(jnp.float32)).astype(jnp.bfloat16)
            if step == 1:
                returning.append(moved(sums[chunk], down(1)))
    if reach == 1:
        returning += [moved(sums[chunk], down(1)) for chunk in each]
    for chunk in each if reach == 1 else each[-1:]:
        own_grads(chunk)

    returning[0], finished[-1] = lax.optimization_barrier((returning[0], finished[-1]))
    kv_swap = [(0, 1), (1, 0)]
    if chunks * lax.axis_size("kv") * HEAD_SIZE > key_matrix.shape[1]:
        key_scale = jnp.where(jnp.arange(2 * rows)[:, None] < rows, scale, 1.0).astype(jnp.float32)
        both = []
        for chunk in each:
            mine = (finished[chunk] + returning[chunk].astype(jnp.float32)).astype(jnp.bfloat16)
            other = lax.ppermute(mine, "kv", kv_swap).astype(jnp.float32)
            both.append(((mine.astype(jnp.float32) + other) * key_scale).astype(jnp.bfloat16))
        both = joined(both, 1)
        return query_grad[0], both[:rows], both[rows:]
    kv_grads, before = (), []
    for chunk in each:
        mine = call(
            functools.partial(finish_kernel, scale=scale),
            (finished[chunk], returning[chunk]),
            (sent_shape,),
            [],
            "finish",
            0.1,
            after=before,
        )[0]
        before = [mine]
        other = lax.ppermute(mine, "kv", kv_swap)
        kv_grads = pl.pallas_call(
            functools.partial(place_kernel, chunk=chunk, chunks=chunks),
            out_shape=(jax.ShapeDtypeStruct(key_matrix.shape, jnp.bfloat16),) * 2,
            in_specs=[WHOLE] * 2 + [ANYWHERE] * len(kv_grads),
            out_specs=(ANYWHERE,) * 2,
            scratch_shapes=[pltpu.SemaphoreType.DMA((2, 2))],
            input_output_aliases={2 + index: index for index in range(len(kv_grads))},
            compiler_params=pltpu.CompilerParams(vmem_limit_bytes=VMEM_LIMIT),
            name="place",
        )(mine, other, *kv_grads)
    return (query_grad[0], *kv_grads)


def solution(mesh):
    return jax.shard_map(
        shards,
        mesh=mesh,
        in_specs=(
            P(("groups", "ctx"), ("tp", "kv")),
            P(("groups", "ctx"), "tp"),
            P(("groups", "ctx"), "tp"),
            P(("groups", "ctx"), ("tp", "kv")),
            P(("groups", "ctx")),
        ),
        out_specs=(
            P(("groups", "ctx"), ("tp", "kv")),
            P(("groups", "ctx"), "tp"),
            P(("groups", "ctx"), "tp"),
        ),
        check_vma=False,
    )
```

```python
import functools
import jax
import jax.numpy as jnp
from jax import lax
from jax.experimental import pallas as pl
from jax.experimental.pallas import tpu as pltpu
from jax.sharding import PartitionSpec as P

QUERY_HEADS = 64
KEY_VALUE_HEADS = 8
HEAD_SIZE = 128
SEGMENT_ROWS = 16
TILE = 32
HINT = 0.2
AHEAD = 3
FILL_LOW = -1e30
LOG2_E = 1.4426950408889634
VMEM_LIMIT = 40 * 1024 * 1024
PACK_VMEM_LIMIT = 53 * 1024 * 1024 + 512 * 1024
LOAD_VMEM_LIMIT = 51 * 1024 * 1024
NUMBER_VMEM_LIMIT = 50 * 1024 * 1024
LOAD_PIECES = 8

WHOLE = pl.BlockSpec(memory_space=pltpu.VMEM)
ANYWHERE = pl.BlockSpec(memory_space=pl.ANY)


def across(a, b):
    return lax.dot_general(a, b, (((1,), (1,)), ((), ())), preferred_element_type=jnp.float32)


def times(a, b):
    return jnp.dot(a, b, preferred_element_type=jnp.float32)


def joined(pieces, axis):
    return pieces[0] if len(pieces) == 1 else jnp.concatenate(pieces, axis=axis)


def pack_kernel(k_ref, v_ref, *refs, first_of):
    *out_refs, sems = refs
    rows = k_ref.shape[0]
    first = first_of(lax.axis_index("kv"))
    copies = []
    for chunk, out_ref in enumerate(out_refs):
        columns = pl.ds(pl.multiple_of((first + chunk) * HEAD_SIZE, HEAD_SIZE), HEAD_SIZE)
        for part, ref in enumerate((k_ref, v_ref)):
            copies.append(
                pltpu.make_async_copy(
                    ref.at[:, columns],
                    out_ref.at[pl.ds(part * rows, rows), :],
                    sems.at[2 * chunk + part],
                )
            )
    for copy in copies:
        copy.start()
    for copy in copies:
        copy.wait()


def number_kernel(seg_ref, own_ref, out_ref):
    rows = seg_ref.shape[1]
    numbers = jnp.broadcast_to(seg_ref[...].astype(jnp.float32) + 1.0, (number_rows(rows), rows))
    pieces = [numbers[:, at : at + HEAD_SIZE] for at in range(0, rows, HEAD_SIZE)]
    tail = joined(pieces, 0).astype(jnp.bfloat16)
    out_ref[: 2 * rows, :] = own_ref[: 2 * rows, :]
    out_ref[pl.ds(2 * rows, tail.shape[0]), :] = tail


def load_kernel(q_ref, g_ref, own_ref, q_out_ref, g_out_ref, sems):
    pieces = sems.shape[1]
    count = q_ref.shape[0] // pieces
    copies = []
    for piece in range(pieces):
        here = slice(piece * count, (piece + 1) * count)
        for part, (ref, out_ref) in enumerate(((q_ref, q_out_ref), (g_ref, g_out_ref))):
            copies.append(
                pltpu.make_async_copy(
                    ref.at[here, :], out_ref.at[here, :], sems.at[part, piece]
                )
            )
    for copy in copies:
        copy.start()
    for copy in copies:
        copy.wait()


def number_rows(rows):
    return max(SEGMENT_ROWS * HEAD_SIZE // rows, 1)


def segment_row(ref, rows):
    repeat = number_rows(rows)
    count = repeat * rows // HEAD_SIZE
    tail = ref[pl.ds(ref.shape[0] - count, count), :].astype(jnp.float32)
    return joined([tail[at : at + 1] for at in range(0, tail.shape[0], repeat)], 1)


def fill_bias(bias_ref, own_ref, kv_ref, step):
    rows = bias_ref.shape[0]
    q_seg = segment_row(own_ref, rows)
    k_seg = segment_row(kv_ref, rows)
    k_col = jnp.broadcast_to(k_seg, (8, rows)).T[:, :1]
    allowed = k_col == q_seg
    if step == 0:
        k_pos = lax.broadcasted_iota(jnp.int32, (rows, rows), 0)
        q_pos = lax.broadcasted_iota(jnp.int32, (rows, rows), 1)
        allowed = allowed & (k_pos <= q_pos)
    bias_ref[...] = jnp.where(allowed, 0.0, FILL_LOW)


def activity(own_ref, kv_ref, step, rows):
    q_seg = segment_row(own_ref, rows)
    k_seg = segment_row(kv_ref, rows)
    reached = lax.axis_index("ctx") >= step
    active = reached & (k_seg[0, rows - 1] >= q_seg[0, 0]) & (k_seg[0, 0] <= q_seg[0, rows - 1])
    return active, k_seg[0, rows // 2 - 1] >= q_seg[0, 0]


def full_units(per_kv, rows):
    return [(slice(0, rows), [(head, slice(0, rows))]) for head in range(per_kv)]


def own_units(per_kv, rows):
    half = rows // 2
    units = []
    for head in range(0, per_kv, 2):
        units += [(slice(0, half), [(head + i, slice(0, rows))]) for i in range(2)]
        units.append((slice(half, rows), [(head + i, slice(half, rows)) for i in range(2)]))
    return units


def late_units(per_kv, rows):
    return [(slice(rows // 2, rows), [(head, slice(0, rows))]) for head in range(per_kv)]


def early_units(per_kv, rows):
    early = slice(0, rows // 2)
    return [(slice(0, rows), [(head, early), (head + 1, early)]) for head in range(0, per_kv, 2)]


class Unit:
    def __init__(self, unit, base, q_ref, g_ref, kv_ref, bias_ref):
        self.keys, self.parts = unit
        self.rows = kv_ref.shape[0] // 2
        self.bias_ref = bias_ref
        rows = bias_ref.shape[0]
        self.q = self.gather(q_ref, base)
        self.g = self.gather(g_ref, base)
        k = kv_ref[self.keys, :]
        v = kv_ref[slice(rows + self.keys.start, rows + self.keys.stop), :]
        self.raw = across(k, self.q)
        self.dprobs = across(v, self.g)

    def gather(self, ref, base):
        return joined(
            [ref[span, (base + head) * HEAD_SIZE : (base + head + 1) * HEAD_SIZE] for head, span in self.parts],
            0,
        )

    def row(self, ref, part):
        return joined([ref[part, head : head + 1, span] for head, span in self.parts], 1)

    def put_row(self, ref, part, value):
        for (head, span), piece in zip(self.parts, self.split(value)):
            ref[part, head : head + 1, span] = piece

    def split(self, value):
        at, pieces = 0, []
        for _, span in self.parts:
            width = span.stop - span.start
            pieces.append(value[:, at : at + width])
            at += width
        return pieces

    def tiles(self):
        for first in range(0, self.keys.stop - self.keys.start, TILE):
            here = slice(first, first + TILE)
            key_rows = slice(self.keys.start + first, self.keys.start + first + TILE)
            bias = joined([self.bias_ref[key_rows, span] for _, span in self.parts], 1)
            yield bias, self.raw[here], self.dprobs[here]

    def updated(self, stats, factor):
        scores, top = [], None
        for bias, raw, _ in self.tiles():
            scores.append(raw * factor + bias)
            top = scores[-1] if top is None else jnp.maximum(top, scores[-1])
        peak = jnp.max(top, axis=0, keepdims=True)
        if stats is not None:
            peak = jnp.maximum(peak, stats[0])
        weights, total, weighted = [], None, None
        for tile, (_, _, dprobs) in zip(scores, self.tiles()):
            weights.append(jnp.exp2(tile - peak))
            product = weights[-1] * dprobs
            total = weights[-1] if total is None else total + weights[-1]
            weighted = product if weighted is None else weighted + product
        total = jnp.sum(total, axis=0, keepdims=True)
        weighted = jnp.sum(weighted, axis=0, keepdims=True)
        if stats is not None:
            fade = jnp.exp2(stats[0] - peak)
            total = total + stats[1] * fade
            weighted = weighted + stats[2] * fade
        return (peak, total, weighted), weights

    def lowered(self, log_total, delta, factor, weights=None, inverse=None):
        probs, dscores = [], []
        for index, (bias, raw, dprobs) in enumerate(self.tiles()):
            if weights is None:
                tile = jnp.exp2(raw * factor + bias - log_total)
            else:
                tile = weights[index] * inverse
            probs.append(tile.astype(jnp.bfloat16))
            dscores.append((tile * (dprobs - delta)).astype(jnp.bfloat16))
        self.probs, self.dscores = joined(probs, 0), joined(dscores, 0)


def in_turn(units, make, handle, count):
    made = [make(unit) for unit in units[:count]]
    for index in range(len(units)):
        if index + count < len(units):
            made.append(make(units[index + count]))
        handle(made[index])
        made[index] = None


class GradSum:
    def __init__(self, acc_ref, rows):
        self.acc_ref, self.rows, self.waiting, self.seen = acc_ref, rows, {}, set()

    def add(self, unit):
        key = unit.keys.start, unit.keys.stop
        self.waiting.setdefault(key, []).append(unit)
        if len(self.waiting[key]) == 2:
            self.flush(key)

    def flush(self, key):
        units = self.waiting.pop(key)
        first, last = key
        for offset, lhs, rhs in (
            (0, joined([u.dscores for u in units], 1), joined([u.q for u in units], 0)),
            (self.rows, joined([u.probs for u in units], 1), joined([u.g for u in units], 0)),
        ):
            here = slice(offset + first, offset + last)
            term = times(lhs, rhs)
            self.acc_ref[here, :] = self.acc_ref[here, :] + term if key in self.seen else term
        self.seen.add(key)

    def finish(self):
        for key in list(self.waiting):
            self.flush(key)


def finals(stats):
    return stats[0] + jnp.log2(stats[1]), stats[2] / stats[1]


def stats_kernel(ins, outs, _, *, fill, chunk, per_kv, factor, step):
    q_ref, g_ref, own_seg_ref, kv_ref, kv_seg_ref = ins[:5]
    in_ref = ins[5] if step else None
    out_ref = outs[0]
    bias_ref = outs[1] if fill else ins[-1]
    rows = q_ref.shape[0]

    def run():
        if fill:
            fill_bias(bias_ref, own_seg_ref, kv_seg_ref, step)

        def handle(unit):
            source = in_ref
            if step == 0:
                source = out_ref if unit.keys.start > 0 else None
            stats = None if source is None else tuple(unit.row(source, part) for part in range(3))
            for part, value in enumerate(unit.updated(stats, factor)[0]):
                unit.put_row(out_ref, part, value)

        units = full_units(per_kv, rows) if step else own_units(per_kv, rows)
        in_turn(units, lambda unit: Unit(unit, chunk * per_kv, q_ref, g_ref, kv_ref, bias_ref), handle, AHEAD)

    if step == 0:
        run()
        return
    active, _ = activity(own_seg_ref, kv_seg_ref, step, rows)
    pl.when(active)(run)

    @pl.when(jnp.logical_not(active))
    def _():
        out_ref[...] = in_ref[...]


def far_kernel(ins, outs, scratch, *, early_own, fill, chunk, per_kv, factor, scale, step):
    q_ref, g_ref, own_seg_ref, kv_ref, kv_seg_ref, in_ref = ins[:6]
    out_ref, kv_grad_ref, dq_ref = outs[:3]
    bias_ref = outs[-1] if fill else ins[-1]
    kt_ref, acc_ref = scratch[:2]
    rows = q_ref.shape[0]
    half = rows // 2
    active, early = activity(own_seg_ref, kv_seg_ref, step, rows)
    log_total, delta = finals((in_ref[0], in_ref[1], in_ref[2]))
    out_ref[0] = log_total
    out_ref[1] = delta

    def run(units, keys):
        if fill:
            fill_bias(bias_ref, own_seg_ref, kv_seg_ref, step)
        kt_ref[...] = kv_ref[:rows, :].T
        if keys.start > 0:
            for offset in (0, rows):
                acc_ref[offset : offset + keys.start, :] = jnp.zeros((keys.start, HEAD_SIZE), jnp.float32)
        grads = GradSum(acc_ref, rows)

        def first(unit):
            stats = tuple(unit.row(in_ref, part) for part in range(3))
            stats, unit.weights = unit.updated(stats, factor)
            unit.finals = finals(stats)
            unit.inverse = 1.0 / stats[1]
            unit.put_row(out_ref, 0, unit.finals[0])
            unit.put_row(out_ref, 1, unit.finals[1])

        def second(unit):
            unit.lowered(*unit.finals, factor, unit.weights, unit.inverse)
            grads.add(unit)
            dq = times(kt_ref[:, unit.keys], unit.dscores)
            for (head, span), piece in zip(unit.parts, unit.split(dq)):
                dq_ref[head, :, span] = piece
                if span.stop < rows:
                    dq_ref[head, :, span.stop :] = jnp.zeros((HEAD_SIZE, rows - span.stop), jnp.float32)

        def both(unit):
            first(unit)
            second(unit)

        def make(unit):
            return Unit(unit, chunk * per_kv, q_ref, g_ref, kv_ref, bias_ref)

        if chunk % 2:
            made = []
            in_turn(units, make, lambda unit: (first(unit), made.append(unit)), AHEAD)
            for unit in made:
                second(unit)
        else:
            in_turn(units, make, both, AHEAD)
        grads.finish()
        kv_grad_ref[...] = acc_ref[...].astype(kv_grad_ref.dtype)

    @pl.when(active & jnp.logical_not(early))
    def _():
        run(late_units(per_kv, rows), slice(half, rows))

    @pl.when(active & early)
    def _():
        run(early_units(per_kv, rows), slice(0, rows))

    @pl.when(jnp.logical_not(active))
    def _():
        dq_ref[...] = jnp.zeros_like(dq_ref)
        kv_grad_ref[...] = jnp.zeros_like(kv_grad_ref)
        if early_own:
            own_kv_ref, near_seg_ref, own_bias_ref = ins[6:9]
            near, _ = activity(own_seg_ref, near_seg_ref, 1, rows)

            @pl.when(jnp.logical_not(near))
            def _():
                own_run(
                    (q_ref, g_ref, own_kv_ref, out_ref, dq_ref, own_bias_ref), outs[3:5],
                    (kt_ref, *scratch[2:]), chunk, per_kv, factor, scale,
                )


def grads_kernel(ins, outs, scratch, *, chunk, per_kv, factor, step):
    q_ref, g_ref, own_seg_ref, kv_ref, kv_seg_ref, in_ref, dq_in_ref, bias_ref = ins
    kv_grad_ref, dq_ref = outs
    kt_ref = scratch[0]
    rows = q_ref.shape[0]

    def make(unit):
        return Unit(unit, chunk * per_kv, q_ref, g_ref, kv_ref, bias_ref)

    def run():
        kt_ref[...] = kv_ref[:rows, :].T
        grads = GradSum(kv_grad_ref, rows)

        def handle(unit):
            unit.lowered(unit.row(in_ref, 0), unit.row(in_ref, 1), factor)
            grads.add(unit)
            head = unit.parts[0][0]
            dq_ref[head] = dq_in_ref[head] + times(kt_ref[:, unit.keys], unit.dscores)

        in_turn(full_units(per_kv, rows), make, handle, AHEAD)
        grads.finish()

    active, _ = activity(own_seg_ref, kv_seg_ref, step, rows)
    pl.when(active)(run)

    @pl.when(jnp.logical_not(active))
    def _():
        kv_grad_ref[...] = jnp.zeros_like(kv_grad_ref)
        dq_ref[...] = dq_in_ref[...]


def own_run(ins, outs, scratch, chunk, per_kv, factor, scale):
    q_ref, g_ref, kv_ref, in_ref, dq_in_ref, bias_ref = ins
    kv_grad_ref, query_grad_ref = outs
    kt_ref, turned_ref, sems = scratch
    rows = q_ref.shape[0]
    half = rows // 2
    kt_ref[...] = kv_ref[:rows, :].T
    grads = GradSum(kv_grad_ref, rows)
    dq_now, copies = {}, []

    def send(head, count):
        here = slice(head * HEAD_SIZE, (head + count) * HEAD_SIZE)
        there = slice((chunk * per_kv + head) * HEAD_SIZE, (chunk * per_kv + head + count) * HEAD_SIZE)
        copies.append(
            pltpu.make_async_copy(turned_ref.at[:, here], query_grad_ref.at[:, there], sems.at[head // count])
        )
        copies[-1].start()

    def handle(unit):
        unit.lowered(unit.row(in_ref, 0), unit.row(in_ref, 1), factor)
        grads.add(unit)
        dq = times(kt_ref[:, unit.keys], unit.dscores)
        head = unit.parts[0][0]
        if unit.keys.start == 0:
            dq_now[head] = dq_in_ref[head] + dq
            return
        for (other, _), piece in zip(unit.parts, unit.split(dq)):
            total = dq_now.pop(other)
            for at, value in ((0, total[:, :half]), (half, total[:, half:] + piece)):
                turned_ref[at : at + half, other * HEAD_SIZE : (other + 1) * HEAD_SIZE] = (
                    (value * scale).astype(jnp.bfloat16).T
                )
        send(head, len(unit.parts))

    def make(unit):
        return Unit(unit, chunk * per_kv, q_ref, g_ref, kv_ref, bias_ref)

    in_turn(own_units(per_kv, rows), make, handle, AHEAD)
    grads.finish()
    for copy in copies:
        copy.wait()


def own_kernel(ins, outs, scratch, *, done_before, chunk, per_kv, factor, scale):
    q_ref, g_ref, own_seg_ref, kv_ref, kv_seg_ref, in_ref, dq_in_ref, bias_ref = ins[:8]

    def run():
        own_run(
            (q_ref, g_ref, kv_ref, in_ref, dq_in_ref, bias_ref), outs, scratch,
            chunk, per_kv, factor, scale,
        )

    if not done_before:
        run()
        return
    active, _ = activity(own_seg_ref, kv_seg_ref, 1, q_ref.shape[0])
    pl.when(active)(run)

    @pl.when(jnp.logical_not(active))
    def _():
        outs[0][...] = ins[8][...]


def finish_kernel(ins, outs, _, *, scale):
    own_ref, arrived_ref = ins
    rows = own_ref.shape[0] // 2
    for first, factor in ((0, scale), (rows, 1.0)):
        here = slice(first, first + rows)
        total = (own_ref[here, :] + arrived_ref[here, :].astype(jnp.float32)) * factor
        outs[0][here, :] = total.astype(jnp.bfloat16)


def place_kernel(mine_ref, other_ref, *refs, chunk, chunks):
    *out_refs, sems = refs[-3:]
    rows = out_refs[0].shape[0]
    core = lax.axis_index("kv")
    copies = []
    for place, ref in enumerate((mine_ref, other_ref)):
        first = ((1 - core if place else core) * chunks + chunk) * HEAD_SIZE
        columns = pl.ds(pl.multiple_of(first, HEAD_SIZE), HEAD_SIZE)
        for part, out_ref in enumerate(out_refs):
            copies.append(
                pltpu.make_async_copy(
                    ref.at[pl.ds(part * rows, rows), :], out_ref.at[:, columns], sems.at[place, part]
                )
            )
    for copy in copies:
        copy.start()
    for copy in copies:
        copy.wait()


def shards(queries, key_matrix, value_matrix, out_grad, segments):
    rows = queries.shape[0]
    heads = queries.shape[1] // HEAD_SIZE
    group_width = QUERY_HEADS // KEY_VALUE_HEADS
    chunks = max(heads // group_width, 1)
    per_kv = heads // chunks
    ctx = lax.axis_size("ctx")
    groups = lax.axis_size("groups")
    longest = rows * ctx // 2
    reach = min(ctx - 1, (longest - 1 + rows - 1) // rows)
    scale = HEAD_SIZE ** (-0.5)
    factor = scale * LOG2_E
    tail = number_rows(rows) * rows // HEAD_SIZE
    block_shapes = tuple(
        jax.ShapeDtypeStruct((2 * rows + (0 if chunk else tail), HEAD_SIZE), jnp.bfloat16)
        for chunk in range(chunks)
    )
    pairs = per_kv * rows * rows
    each = range(chunks)

    def first_of(kv_index):
        return kv_index * heads // group_width

    def up(step):
        route = []
        for group in range(groups):
            at = group * ctx
            beside = (group + 1) % groups * ctx
            route += [(at + i, beside + i) for i in range(step - 1)]
            route += [(at + i, at + i + 1) for i in range(step - 1, ctx - 1)]
            route.append((at + ctx - 1, at + step - 1))
        return route

    def down(step):
        return [(target, source) for source, target in up(step)]

    def moved(array, route):
        return lax.ppermute(array, ("groups", "ctx"), route)

    def call(body, operands, outs, scratch, name, micros, out_specs=None, into=(), after=()):
        count = len(operands)
        extra = [array for array, _ in into] + list(after)
        specs = [out_specs[index] for _, index in into] + [ANYWHERE] * len(after)

        def kernel(*refs):
            rest = refs[count + len(extra) :]
            body(refs[:count], rest[: len(outs)], rest[len(outs) :])

        return pl.pallas_call(
            kernel,
            out_shape=outs,
            in_specs=[WHOLE] * count + specs,
            out_specs=out_specs or (WHOLE,) * len(outs),
            scratch_shapes=scratch,
            input_output_aliases={count + place: index for place, (_, index) in enumerate(into)},
            compiler_params=pltpu.CompilerParams(vmem_limit_bytes=VMEM_LIMIT),
            cost_estimate=pl.CostEstimate(
                flops=int(1153e6 * micros * HINT), bytes_accessed=4 * pairs // rows, transcendentals=pairs
            ),
            name=name,
        )(*operands, *extra)

    own = pl.pallas_call(
        functools.partial(pack_kernel, first_of=first_of),
        out_shape=block_shapes,
        in_specs=[ANYWHERE] * 2,
        out_specs=(WHOLE,) * chunks,
        scratch_shapes=[pltpu.SemaphoreType.DMA((2 * chunks,))],
        compiler_params=pltpu.CompilerParams(vmem_limit_bytes=PACK_VMEM_LIMIT),
        cost_estimate=pl.CostEstimate(flops=0, bytes_accessed=4 * 1024 * 1024, transcendentals=0),
        name="pack",
    )(key_matrix, value_matrix)
    own = list(own)
    own[0] = pl.pallas_call(
        number_kernel,
        out_shape=block_shapes[0],
        in_specs=[WHOLE] * 2,
        out_specs=WHOLE,
        input_output_aliases={1: 0},
        compiler_params=pltpu.CompilerParams(vmem_limit_bytes=NUMBER_VMEM_LIMIT),
        name="number",
    )(segments.reshape(1, rows), own[0])

    rows_shape = jax.ShapeDtypeStruct(queries.shape, jnp.bfloat16)
    queries, out_grad = pl.pallas_call(
        load_kernel,
        out_shape=(rows_shape, rows_shape),
        in_specs=[ANYWHERE] * 3,
        out_specs=(WHOLE, WHOLE),
        scratch_shapes=[pltpu.SemaphoreType.DMA((2, LOAD_PIECES))],
        compiler_params=pltpu.CompilerParams(vmem_limit_bytes=LOAD_VMEM_LIMIT),
        name="load",
    )(queries, out_grad, own[0])

    turned = pltpu.VMEM((HEAD_SIZE, rows), jnp.bfloat16)
    total_sum = pltpu.VMEM((2 * rows, HEAD_SIZE), jnp.float32)
    bias_shape = jax.ShapeDtypeStruct((rows, rows), jnp.float32)
    stats_shape = jax.ShapeDtypeStruct((3, per_kv, rows), jnp.float32)
    finals_shape = jax.ShapeDtypeStruct((2, per_kv, rows), jnp.float32)
    dq_shape = jax.ShapeDtypeStruct((per_kv, HEAD_SIZE, rows), jnp.float32)
    kv_grad_shape = jax.ShapeDtypeStruct((2 * rows, HEAD_SIZE), jnp.float32)
    sent_shape = jax.ShapeDtypeStruct((2 * rows, HEAD_SIZE), jnp.bfloat16)
    common = {"per_kv": per_kv, "factor": factor}
    biases = [None] * (reach + 1)
    own = list(lax.optimization_barrier(tuple(own)))
    blocks = [[own[chunk], moved(own[chunk], up(1))] for chunk in each]

    def common_operands(chunk, step):
        return queries, out_grad, own[0], blocks[chunk][step], blocks[0][step]

    def with_bias(kernel, chunk, step, operands, outs, scratch, name, micros, after=(), specs=None, **options):
        fill = biases[step] is None
        body = functools.partial(kernel, fill=fill, chunk=chunk, step=step, **options, **common)
        operands = common_operands(chunk, step) + operands
        specs = specs or (WHOLE,) * len(outs)
        if not fill:
            return call(body, operands + (biases[step],), outs, scratch, name, micros, specs, after=after)
        *results, biases[step] = call(
            body, operands, outs + (bias_shape,), scratch, name, micros, specs + (WHOLE,), after=after
        )
        return results

    stats, final_stats = [None] * chunks, [None] * chunks
    sums, dq = [None] * chunks, [None] * chunks
    for chunk in each:
        after = [blocks[chunk - 1][1]] if chunk else []
        (stats[chunk],) = with_bias(
            stats_kernel, chunk, 0, (), (stats_shape,), [], "stats_own", 0.8, after
        )
    for step in range(1, reach):
        for chunk in each:
            here, stats[chunk] = lax.optimization_barrier((blocks[chunk][step], stats[chunk]))
            blocks[chunk].append(moved(here, up(step + 1)))
        for chunk in each:
            (stats[chunk],) = with_bias(
                stats_kernel, chunk, step, (stats[chunk],), (stats_shape,), [], "stats", 1.1
            )
    finished, returning, query_grad = [None] * chunks, [], []
    own_outs = (kv_grad_shape, jax.ShapeDtypeStruct(queries.shape, jnp.bfloat16))
    own_specs = (WHOLE, ANYWHERE)
    written_scratch = [
        pltpu.VMEM((rows, per_kv * HEAD_SIZE), jnp.bfloat16),
        pltpu.SemaphoreType.DMA((per_kv // 2,)),
    ]
    own_scratch = [turned] + written_scratch

    def far_grads(chunk, before):
        operands = (stats[chunk],)
        outs, specs, scratch = (finals_shape, sent_shape, dq_shape), (WHOLE,) * 3, [turned, total_sum]
        early_own = chunk == 0
        if early_own:
            operands += (own[chunk], blocks[0][1], biases[0])
            outs, specs, scratch = outs + own_outs, specs + own_specs, scratch + written_scratch
        final_stats[chunk], sums[chunk], dq[chunk], *rest = with_bias(
            far_kernel, chunk, reach, operands, outs, scratch, "grads_far", 1.3, before, specs,
            early_own=early_own, scale=scale,
        )
        if early_own:
            finished[chunk] = rest[0]
            query_grad.append(rest[1])
        return [sums[chunk]]

    def block_grads(chunk, step, before):
        body = functools.partial(grads_kernel, chunk=chunk, step=step, **common)
        operands = common_operands(chunk, step) + (final_stats[chunk], dq[chunk], biases[step])
        mine[chunk], dq[chunk] = call(
            body, operands, (kv_grad_shape, dq_shape), [turned], "grads", 1.6, after=before
        )
        return [mine[chunk]]

    def own_grads(chunk):
        done_before = finished[chunk] is not None
        body = functools.partial(own_kernel, done_before=done_before, chunk=chunk, scale=scale, **common)
        into = [(query_grad.pop(), 1)] if query_grad else []
        seen = 1 if done_before else 0
        finished[chunk], written = call(
            body,
            (queries, out_grad, own[0], blocks[chunk][0], blocks[0][seen])
            + (final_stats[chunk], dq[chunk], biases[0])
            + ((finished[chunk],) if done_before else ()),
            own_outs,
            own_scratch,
            "grads_own",
            1.8,
            out_specs=own_specs,
            into=into,
            after=[sums[chunk]],
        )
        query_grad.append(written)

    mine, arriving = [None] * chunks, [None] * chunks
    before = [stats[-1]]
    for chunk in each:
        before = far_grads(chunk, before)
        arriving[chunk] = moved(sums[chunk], down(reach))
        if reach > 1:
            before = block_grads(chunk, reach - 1, before)
    for step in range(reach - 1, 0, -1):
        if step + 1 < reach:
            arriving = [moved(sums[chunk], down(step + 1)) for chunk in each]
            for chunk in each:
                before = block_grads(chunk, step, before)
        arriving[0], mine[-1] = lax.optimization_barrier((arriving[0], mine[-1]))
        for chunk in each:
            here = arriving[chunk]
            if step == 1 and chunk:
                own_grads(chunk - 1)
                here, finished[chunk - 1] = lax.optimization_barrier((here, finished[chunk - 1]))
            sums[chunk] = (mine[chunk] + here.astype(jnp.float32)).astype(jnp.bfloat16)
            if step == 1:
                returning.append(moved(sums[chunk], down(1)))
    if reach == 1:
        returning += arriving
    for chunk in each if reach == 1 else each[-1:]:
        own_grads(chunk)

    returning[0], finished[-1] = lax.optimization_barrier((returning[0], finished[-1]))
    kv_swap = [(0, 1), (1, 0)]
    if chunks * lax.axis_size("kv") * HEAD_SIZE > key_matrix.shape[1]:
        key_scale = jnp.where(jnp.arange(2 * rows)[:, None] < rows, scale, 1.0).astype(jnp.float32)
        both = []
        for chunk in each:
            mine = (finished[chunk] + returning[chunk].astype(jnp.float32)).astype(jnp.bfloat16)
            other = lax.ppermute(mine, "kv", kv_swap).astype(jnp.float32)
            both.append(((mine.astype(jnp.float32) + other) * key_scale).astype(jnp.bfloat16))
        both = joined(both, 1)
        return query_grad[0], both[:rows], both[rows:]
    kv_grads, before = (), []
    for chunk in each:
        mine = call(
            functools.partial(finish_kernel, scale=scale),
            (finished[chunk], returning[chunk]),
            (sent_shape,),
            [],
            "finish",
            0.1,
            after=before,
        )[0]
        before = [mine]
        other = lax.ppermute(mine, "kv", kv_swap)
        kv_grads = pl.pallas_call(
            functools.partial(place_kernel, chunk=chunk, chunks=chunks),
            out_shape=(jax.ShapeDtypeStruct(key_matrix.shape, jnp.bfloat16),) * 2,
            in_specs=[WHOLE] * 2 + [ANYWHERE] * len(kv_grads),
            out_specs=(ANYWHERE,) * 2,
            scratch_shapes=[pltpu.SemaphoreType.DMA((2, 2))],
            input_output_aliases={2 + index: index for index in range(len(kv_grads))},
            compiler_params=pltpu.CompilerParams(vmem_limit_bytes=VMEM_LIMIT),
            name="place",
        )(mine, other, *kv_grads)
    return (query_grad[0], *kv_grads)


def solution(mesh):
    return jax.shard_map(
        shards,
        mesh=mesh,
        in_specs=(
            P(("groups", "ctx"), ("tp", "kv")),
            P(("groups", "ctx"), "tp"),
            P(("groups", "ctx"), "tp"),
            P(("groups", "ctx"), ("tp", "kv")),
            P(("groups", "ctx")),
        ),
        out_specs=(
            P(("groups", "ctx"), ("tp", "kv")),
            P(("groups", "ctx"), "tp"),
            P(("groups", "ctx"), "tp"),
        ),
        check_vma=False,
    )
```

```python
import functools
import jax
import jax.numpy as jnp
from jax import lax
from jax.experimental import pallas as pl
from jax.experimental.pallas import tpu as pltpu
from jax.sharding import PartitionSpec as P

QUERY_HEADS = 64
KEY_VALUE_HEADS = 8
HEAD_SIZE = 128
SEGMENT_ROWS = 16
TILE = 32
HINT = 0.2
AHEAD = 3
FILL_LOW = -1e30
LOG2_E = 1.4426950408889634
VMEM_LIMIT = 40 * 1024 * 1024
PACK_VMEM_LIMIT = 53 * 1024 * 1024 + 512 * 1024
LOAD_VMEM_LIMIT = 51 * 1024 * 1024
NUMBER_VMEM_LIMIT = 50 * 1024 * 1024
LOAD_PIECES = 8

WHOLE = pl.BlockSpec(memory_space=pltpu.VMEM)
ANYWHERE = pl.BlockSpec(memory_space=pl.ANY)


def across(a, b):
    return lax.dot_general(a, b, (((1,), (1,)), ((), ())), preferred_element_type=jnp.float32)


def times(a, b):
    return jnp.dot(a, b, preferred_element_type=jnp.float32)


def joined(pieces, axis):
    return pieces[0] if len(pieces) == 1 else jnp.concatenate(pieces, axis=axis)


def pack_kernel(k_ref, v_ref, *refs, first_of):
    *out_refs, sems = refs
    rows = k_ref.shape[0]
    first = first_of(lax.axis_index("kv"))
    copies = []
    for chunk, out_ref in enumerate(out_refs):
        columns = pl.ds(pl.multiple_of((first + chunk) * HEAD_SIZE, HEAD_SIZE), HEAD_SIZE)
        for part, ref in enumerate((k_ref, v_ref)):
            copies.append(
                pltpu.make_async_copy(
                    ref.at[:, columns],
                    out_ref.at[pl.ds(part * rows, rows), :],
                    sems.at[2 * chunk + part],
                )
            )
    for copy in copies:
        copy.start()
    for copy in copies:
        copy.wait()


def number_kernel(seg_ref, own_ref, out_ref):
    rows = seg_ref.shape[1]
    numbers = jnp.broadcast_to(seg_ref[...].astype(jnp.float32) + 1.0, (number_rows(rows), rows))
    pieces = [numbers[:, at : at + HEAD_SIZE] for at in range(0, rows, HEAD_SIZE)]
    tail = joined(pieces, 0).astype(jnp.bfloat16)
    out_ref[: 2 * rows, :] = own_ref[: 2 * rows, :]
    out_ref[pl.ds(2 * rows, tail.shape[0]), :] = tail


def load_kernel(q_ref, g_ref, own_ref, q_out_ref, g_out_ref, sems):
    pieces = sems.shape[1]
    count = q_ref.shape[0] // pieces
    copies = []
    for piece in range(pieces):
        here = slice(piece * count, (piece + 1) * count)
        for part, (ref, out_ref) in enumerate(((q_ref, q_out_ref), (g_ref, g_out_ref))):
            copies.append(
                pltpu.make_async_copy(
                    ref.at[here, :], out_ref.at[here, :], sems.at[part, piece]
                )
            )
    for copy in copies:
        copy.start()
    for copy in copies:
        copy.wait()


def number_rows(rows):
    return max(SEGMENT_ROWS * HEAD_SIZE // rows, 1)


def segment_row(ref, rows):
    repeat = number_rows(rows)
    count = repeat * rows // HEAD_SIZE
    tail = ref[pl.ds(ref.shape[0] - count, count), :].astype(jnp.float32)
    return joined([tail[at : at + 1] for at in range(0, tail.shape[0], repeat)], 1)


def fill_bias(bias_ref, own_ref, kv_ref, step):
    rows = bias_ref.shape[0]
    q_seg = segment_row(own_ref, rows)
    k_seg = segment_row(kv_ref, rows)
    k_col = jnp.broadcast_to(k_seg, (8, rows)).T[:, :1]
    allowed = k_col == q_seg
    if step == 0:
        k_pos = lax.broadcasted_iota(jnp.int32, (rows, rows), 0)
        q_pos = lax.broadcasted_iota(jnp.int32, (rows, rows), 1)
        allowed = allowed & (k_pos <= q_pos)
    bias_ref[...] = jnp.where(allowed, 0.0, FILL_LOW)


def activity(own_ref, kv_ref, step, rows):
    q_seg = segment_row(own_ref, rows)
    k_seg = segment_row(kv_ref, rows)
    reached = lax.axis_index("ctx") >= step
    first = q_seg[0, 0]
    return reached & (k_seg[0, rows - 1] >= first), k_seg[0, rows // 2 - 1] >= first


def full_units(per_kv, rows):
    return [(slice(0, rows), [(head, slice(0, rows))]) for head in range(per_kv)]


def own_units(per_kv, rows):
    half = rows // 2
    units = []
    for head in range(0, per_kv, 2):
        units += [(slice(0, half), [(head + i, slice(0, rows))]) for i in range(2)]
        units.append((slice(half, rows), [(head + i, slice(half, rows)) for i in range(2)]))
    return units


def late_units(per_kv, rows):
    return [(slice(rows // 2, rows), [(head, slice(0, rows))]) for head in range(per_kv)]


def early_units(per_kv, rows):
    early = slice(0, rows // 2)
    return [(slice(0, rows), [(head, early), (head + 1, early)]) for head in range(0, per_kv, 2)]


class Unit:
    def __init__(self, unit, base, q_ref, g_ref, kv_ref, bias_ref):
        self.keys, self.parts = unit
        self.rows = kv_ref.shape[0] // 2
        self.bias_ref = bias_ref
        rows = bias_ref.shape[0]
        self.q = self.gather(q_ref, base)
        self.g = self.gather(g_ref, base)
        k = kv_ref[self.keys, :]
        v = kv_ref[slice(rows + self.keys.start, rows + self.keys.stop), :]
        self.raw = across(k, self.q)
        self.dprobs = across(v, self.g)

    def gather(self, ref, base):
        return joined(
            [ref[span, (base + head) * HEAD_SIZE : (base + head + 1) * HEAD_SIZE] for head, span in self.parts],
            0,
        )

    def row(self, ref, part):
        return joined([ref[part, head : head + 1, span] for head, span in self.parts], 1)

    def put_row(self, ref, part, value):
        for (head, span), piece in zip(self.parts, self.split(value)):
            ref[part, head : head + 1, span] = piece

    def split(self, value):
        at, pieces = 0, []
        for _, span in self.parts:
            width = span.stop - span.start
            pieces.append(value[:, at : at + width])
            at += width
        return pieces

    def tiles(self):
        for first in range(0, self.keys.stop - self.keys.start, TILE):
            here = slice(first, first + TILE)
            key_rows = slice(self.keys.start + first, self.keys.start + first + TILE)
            bias = joined([self.bias_ref[key_rows, span] for _, span in self.parts], 1)
            yield bias, self.raw[here], self.dprobs[here]

    def updated(self, stats, factor):
        scores, top = [], None
        for bias, raw, _ in self.tiles():
            scores.append(raw * factor + bias)
            top = scores[-1] if top is None else jnp.maximum(top, scores[-1])
        peak = jnp.max(top, axis=0, keepdims=True)
        if stats is not None:
            peak = jnp.maximum(peak, stats[0])
        weights, total, weighted = [], None, None
        for tile, (_, _, dprobs) in zip(scores, self.tiles()):
            weights.append(jnp.exp2(tile - peak))
            product = weights[-1] * dprobs
            total = weights[-1] if total is None else total + weights[-1]
            weighted = product if weighted is None else weighted + product
        total = jnp.sum(total, axis=0, keepdims=True)
        weighted = jnp.sum(weighted, axis=0, keepdims=True)
        if stats is not None:
            fade = jnp.exp2(stats[0] - peak)
            total = total + stats[1] * fade
            weighted = weighted + stats[2] * fade
        return (peak, total, weighted), weights

    def lowered(self, log_total, delta, factor, weights=None, inverse=None):
        probs, dscores = [], []
        for index, (bias, raw, dprobs) in enumerate(self.tiles()):
            if weights is None:
                tile = jnp.exp2(raw * factor + bias - log_total)
            else:
                tile = weights[index] * inverse
            probs.append(tile.astype(jnp.bfloat16))
            dscores.append((tile * (dprobs - delta)).astype(jnp.bfloat16))
        self.probs, self.dscores = joined(probs, 0), joined(dscores, 0)


def in_turn(units, make, handle, count):
    made = [make(unit) for unit in units[:count]]
    for index in range(len(units)):
        if index + count < len(units):
            made.append(make(units[index + count]))
        handle(made[index])
        made[index] = None


class GradSum:
    def __init__(self, acc_ref, rows):
        self.acc_ref, self.rows, self.waiting, self.seen = acc_ref, rows, {}, set()

    def add(self, unit):
        key = unit.keys.start, unit.keys.stop
        self.waiting.setdefault(key, []).append(unit)
        if len(self.waiting[key]) == 4:
            self.flush(key)

    def flush(self, key):
        units = self.waiting.pop(key)
        first, last = key
        for offset, lhs, rhs in (
            (0, joined([u.dscores for u in units], 1), joined([u.q for u in units], 0)),
            (self.rows, joined([u.probs for u in units], 1), joined([u.g for u in units], 0)),
        ):
            here = slice(offset + first, offset + last)
            term = times(lhs, rhs)
            self.acc_ref[here, :] = self.acc_ref[here, :] + term if key in self.seen else term
        self.seen.add(key)

    def finish(self):
        for key in list(self.waiting):
            self.flush(key)


def finals(stats):
    return stats[0] + jnp.log2(stats[1]), stats[2] / stats[1]


def stats_kernel(ins, outs, _, *, fill, chunk, per_kv, factor, step):
    q_ref, g_ref, own_seg_ref, kv_ref, kv_seg_ref = ins[:5]
    in_ref = ins[5] if step else None
    out_ref = outs[0]
    bias_ref = outs[1] if fill else ins[-1]
    rows = q_ref.shape[0]

    def run():
        if fill:
            fill_bias(bias_ref, own_seg_ref, kv_seg_ref, step)

        def handle(unit):
            source = in_ref
            if step == 0:
                source = out_ref if unit.keys.start > 0 else None
            stats = None if source is None else tuple(unit.row(source, part) for part in range(3))
            for part, value in enumerate(unit.updated(stats, factor)[0]):
                unit.put_row(out_ref, part, value)

        units = full_units(per_kv, rows) if step else own_units(per_kv, rows)
        in_turn(units, lambda unit: Unit(unit, chunk * per_kv, q_ref, g_ref, kv_ref, bias_ref), handle, AHEAD)

    if step == 0:
        run()
        return
    active, _ = activity(own_seg_ref, kv_seg_ref, step, rows)
    pl.when(active)(run)

    @pl.when(jnp.logical_not(active))
    def _():
        out_ref[...] = in_ref[...]


def far_kernel(ins, outs, scratch, *, early_own, fill, chunk, per_kv, factor, scale, step):
    q_ref, g_ref, own_seg_ref, kv_ref, kv_seg_ref, in_ref = ins[:6]
    out_ref, kv_grad_ref, dq_ref = outs[:3]
    bias_ref = outs[-1] if fill else ins[-1]
    kt_ref, acc_ref = scratch[:2]
    rows = q_ref.shape[0]
    half = rows // 2
    active, early = activity(own_seg_ref, kv_seg_ref, step, rows)
    log_total, delta = finals((in_ref[0], in_ref[1], in_ref[2]))
    out_ref[0] = log_total
    out_ref[1] = delta

    def run(units, keys):
        if fill:
            fill_bias(bias_ref, own_seg_ref, kv_seg_ref, step)
        kt_ref[...] = kv_ref[:rows, :].T
        if keys.start > 0:
            for offset in (0, rows):
                acc_ref[offset : offset + keys.start, :] = jnp.zeros((keys.start, HEAD_SIZE), jnp.float32)
        grads = GradSum(acc_ref, rows)

        def first(unit):
            stats = tuple(unit.row(in_ref, part) for part in range(3))
            stats, unit.weights = unit.updated(stats, factor)
            unit.finals = finals(stats)
            unit.inverse = 1.0 / stats[1]
            unit.put_row(out_ref, 0, unit.finals[0])
            unit.put_row(out_ref, 1, unit.finals[1])

        def second(unit):
            unit.lowered(*unit.finals, factor, unit.weights, unit.inverse)
            grads.add(unit)
            dq = times(kt_ref[:, unit.keys], unit.dscores)
            for (head, span), piece in zip(unit.parts, unit.split(dq)):
                dq_ref[head, :, span] = piece
                if span.stop < rows:
                    dq_ref[head, :, span.stop :] = jnp.zeros((HEAD_SIZE, rows - span.stop), jnp.float32)

        def both(unit):
            first(unit)
            second(unit)

        def make(unit):
            return Unit(unit, chunk * per_kv, q_ref, g_ref, kv_ref, bias_ref)

        if chunk % 2:
            made = []
            in_turn(units, make, lambda unit: (first(unit), made.append(unit)), AHEAD)
            for unit in made:
                second(unit)
        else:
            in_turn(units, make, both, AHEAD)
        grads.finish()
        kv_grad_ref[...] = acc_ref[...].astype(kv_grad_ref.dtype)

    @pl.when(active & jnp.logical_not(early))
    def _():
        run(late_units(per_kv, rows), slice(half, rows))

    @pl.when(active & early)
    def _():
        run(early_units(per_kv, rows), slice(0, rows))

    @pl.when(jnp.logical_not(active))
    def _():
        dq_ref[...] = jnp.zeros_like(dq_ref)
        kv_grad_ref[...] = jnp.zeros_like(kv_grad_ref)
        if early_own:
            own_kv_ref, near_seg_ref, own_bias_ref = ins[6:9]
            near, _ = activity(own_seg_ref, near_seg_ref, 1, rows)

            @pl.when(jnp.logical_not(near))
            def _():
                own_run(
                    (q_ref, g_ref, own_kv_ref, out_ref, dq_ref, own_bias_ref), outs[3:5],
                    (kt_ref, *scratch[2:]), chunk, per_kv, factor, scale,
                )


def grads_kernel(ins, outs, scratch, *, early_own, chunk, per_kv, factor, scale, step):
    q_ref, g_ref, own_seg_ref, kv_ref, kv_seg_ref, in_ref, dq_in_ref, bias_ref = ins[:8]
    kv_grad_ref, dq_ref = outs[:2]
    kt_ref = scratch[0]
    rows = q_ref.shape[0]

    def make(unit):
        return Unit(unit, chunk * per_kv, q_ref, g_ref, kv_ref, bias_ref)

    def run():
        kt_ref[...] = kv_ref[:rows, :].T
        grads = GradSum(kv_grad_ref, rows)

        def handle(unit):
            unit.lowered(unit.row(in_ref, 0), unit.row(in_ref, 1), factor)
            grads.add(unit)
            head = unit.parts[0][0]
            dq_ref[head] = dq_in_ref[head] + times(kt_ref[:, unit.keys], unit.dscores)

        in_turn(full_units(per_kv, rows), make, handle, AHEAD)
        grads.finish()

    active, _ = activity(own_seg_ref, kv_seg_ref, step, rows)
    pl.when(active)(run)

    @pl.when(jnp.logical_not(active))
    def _():
        kv_grad_ref[...] = jnp.zeros_like(kv_grad_ref)
        dq_ref[...] = dq_in_ref[...]
        if early_own:
            own_kv_ref, own_in_ref, own_dq_ref, own_bias_ref = ins[8:]
            own_run(
                (q_ref, g_ref, own_kv_ref, own_in_ref, own_dq_ref, own_bias_ref), outs[2:], scratch,
                chunk + 1, per_kv, factor, scale,
            )


def own_run(ins, outs, scratch, chunk, per_kv, factor, scale):
    q_ref, g_ref, kv_ref, in_ref, dq_in_ref, bias_ref = ins
    kv_grad_ref, query_grad_ref = outs
    kt_ref, turned_ref, sems = scratch
    rows = q_ref.shape[0]
    half = rows // 2
    kt_ref[...] = kv_ref[:rows, :].T
    grads = GradSum(kv_grad_ref, rows)
    dq_now, copies = {}, []

    def send(head, count):
        here = slice(head * HEAD_SIZE, (head + count) * HEAD_SIZE)
        there = slice((chunk * per_kv + head) * HEAD_SIZE, (chunk * per_kv + head + count) * HEAD_SIZE)
        copies.append(
            pltpu.make_async_copy(turned_ref.at[:, here], query_grad_ref.at[:, there], sems.at[head // count])
        )
        copies[-1].start()

    def handle(unit):
        unit.lowered(unit.row(in_ref, 0), unit.row(in_ref, 1), factor)
        grads.add(unit)
        dq = times(kt_ref[:, unit.keys], unit.dscores)
        head = unit.parts[0][0]
        if unit.keys.start == 0:
            dq_now[head] = dq_in_ref[head] + dq
            return
        for (other, _), piece in zip(unit.parts, unit.split(dq)):
            total = dq_now.pop(other)
            for at, value in ((0, total[:, :half]), (half, total[:, half:] + piece)):
                turned_ref[at : at + half, other * HEAD_SIZE : (other + 1) * HEAD_SIZE] = (
                    (value * scale).astype(jnp.bfloat16).T
                )
        send(head, len(unit.parts))

    def make(unit):
        return Unit(unit, chunk * per_kv, q_ref, g_ref, kv_ref, bias_ref)

    in_turn(own_units(per_kv, rows), make, handle, AHEAD)
    grads.finish()
    for copy in copies:
        copy.wait()


def own_kernel(ins, outs, scratch, *, done_before, chunk, per_kv, factor, scale):
    q_ref, g_ref, own_seg_ref, kv_ref, kv_seg_ref, in_ref, dq_in_ref, bias_ref = ins[:8]

    def run():
        own_run(
            (q_ref, g_ref, kv_ref, in_ref, dq_in_ref, bias_ref), outs, scratch,
            chunk, per_kv, factor, scale,
        )

    if not done_before:
        run()
        return
    active, _ = activity(own_seg_ref, kv_seg_ref, 1, q_ref.shape[0])
    pl.when(active)(run)

    @pl.when(jnp.logical_not(active))
    def _():
        outs[0][...] = ins[8][...]


def finish_kernel(ins, outs, _, *, scale):
    own_ref, arrived_ref = ins
    rows = own_ref.shape[0] // 2
    for first, factor in ((0, scale), (rows, 1.0)):
        here = slice(first, first + rows)
        total = (own_ref[here, :] + arrived_ref[here, :].astype(jnp.float32)) * factor
        outs[0][here, :] = total.astype(jnp.bfloat16)


def place_kernel(mine_ref, other_ref, *refs, chunk, chunks):
    *out_refs, sems = refs[-3:]
    rows = out_refs[0].shape[0]
    core = lax.axis_index("kv")
    copies = []
    for place, ref in enumerate((mine_ref, other_ref)):
        first = ((1 - core if place else core) * chunks + chunk) * HEAD_SIZE
        columns = pl.ds(pl.multiple_of(first, HEAD_SIZE), HEAD_SIZE)
        for part, out_ref in enumerate(out_refs):
            copies.append(
                pltpu.make_async_copy(
                    ref.at[pl.ds(part * rows, rows), :], out_ref.at[:, columns], sems.at[place, part]
                )
            )
    for copy in copies:
        copy.start()
    for copy in copies:
        copy.wait()


def shards(queries, key_matrix, value_matrix, out_grad, segments):
    rows = queries.shape[0]
    heads = queries.shape[1] // HEAD_SIZE
    group_width = QUERY_HEADS // KEY_VALUE_HEADS
    chunks = max(heads // group_width, 1)
    per_kv = heads // chunks
    ctx = lax.axis_size("ctx")
    groups = lax.axis_size("groups")
    longest = rows * ctx // 2
    reach = min(ctx - 1, (longest - 1 + rows - 1) // rows)
    scale = HEAD_SIZE ** (-0.5)
    factor = scale * LOG2_E
    tail = number_rows(rows) * rows // HEAD_SIZE
    block_shapes = tuple(
        jax.ShapeDtypeStruct((2 * rows + (0 if chunk else tail), HEAD_SIZE), jnp.bfloat16)
        for chunk in range(chunks)
    )
    pairs = per_kv * rows * rows
    each = range(chunks)

    def first_of(kv_index):
        return kv_index * heads // group_width

    def up(step):
        route = []
        for group in range(groups):
            at = group * ctx
            beside = (group + 1) % groups * ctx
            route += [(at + i, beside + i) for i in range(step - 1)]
            route += [(at + i, at + i + 1) for i in range(step - 1, ctx - 1)]
            route.append((at + ctx - 1, at + step - 1))
        return route

    def down(step):
        return [(target, source) for source, target in up(step)]

    def moved(array, route):
        return lax.ppermute(array, ("groups", "ctx"), route)

    def call(body, operands, outs, scratch, name, micros, out_specs=None, into=(), after=()):
        count = len(operands)
        extra = [array for array, _ in into] + list(after)
        specs = [out_specs[index] for _, index in into] + [ANYWHERE] * len(after)

        def kernel(*refs):
            rest = refs[count + len(extra) :]
            body(refs[:count], rest[: len(outs)], rest[len(outs) :])

        return pl.pallas_call(
            kernel,
            out_shape=outs,
            in_specs=[WHOLE] * count + specs,
            out_specs=out_specs or (WHOLE,) * len(outs),
            scratch_shapes=scratch,
            input_output_aliases={count + place: index for place, (_, index) in enumerate(into)},
            compiler_params=pltpu.CompilerParams(vmem_limit_bytes=VMEM_LIMIT),
            cost_estimate=pl.CostEstimate(
                flops=int(1153e6 * micros * HINT), bytes_accessed=4 * pairs // rows, transcendentals=pairs
            ),
            name=name,
        )(*operands, *extra)

    own = pl.pallas_call(
        functools.partial(pack_kernel, first_of=first_of),
        out_shape=block_shapes,
        in_specs=[ANYWHERE] * 2,
        out_specs=(WHOLE,) * chunks,
        scratch_shapes=[pltpu.SemaphoreType.DMA((2 * chunks,))],
        compiler_params=pltpu.CompilerParams(vmem_limit_bytes=PACK_VMEM_LIMIT),
        cost_estimate=pl.CostEstimate(flops=0, bytes_accessed=4 * 1024 * 1024, transcendentals=0),
        name="pack",
    )(key_matrix, value_matrix)
    own = list(own)
    own[0] = pl.pallas_call(
        number_kernel,
        out_shape=block_shapes[0],
        in_specs=[WHOLE] * 2,
        out_specs=WHOLE,
        input_output_aliases={1: 0},
        compiler_params=pltpu.CompilerParams(vmem_limit_bytes=NUMBER_VMEM_LIMIT),
        name="number",
    )(segments.reshape(1, rows), own[0])

    rows_shape = jax.ShapeDtypeStruct(queries.shape, jnp.bfloat16)
    queries, out_grad = pl.pallas_call(
        load_kernel,
        out_shape=(rows_shape, rows_shape),
        in_specs=[ANYWHERE] * 3,
        out_specs=(WHOLE, WHOLE),
        scratch_shapes=[pltpu.SemaphoreType.DMA((2, LOAD_PIECES))],
        compiler_params=pltpu.CompilerParams(vmem_limit_bytes=LOAD_VMEM_LIMIT),
        name="load",
    )(queries, out_grad, own[0])

    turned = pltpu.VMEM((HEAD_SIZE, rows), jnp.bfloat16)
    total_sum = pltpu.VMEM((2 * rows, HEAD_SIZE), jnp.float32)
    bias_shape = jax.ShapeDtypeStruct((rows, rows), jnp.float32)
    stats_shape = jax.ShapeDtypeStruct((3, per_kv, rows), jnp.float32)
    finals_shape = jax.ShapeDtypeStruct((2, per_kv, rows), jnp.float32)
    dq_shape = jax.ShapeDtypeStruct((per_kv, HEAD_SIZE, rows), jnp.float32)
    kv_grad_shape = jax.ShapeDtypeStruct((2 * rows, HEAD_SIZE), jnp.float32)
    sent_shape = jax.ShapeDtypeStruct((2 * rows, HEAD_SIZE), jnp.bfloat16)
    common = {"per_kv": per_kv, "factor": factor}
    biases = [None] * (reach + 1)
    own = list(lax.optimization_barrier(tuple(own)))
    blocks = [[own[chunk], moved(own[chunk], up(1))] for chunk in each]

    def common_operands(chunk, step):
        return queries, out_grad, own[0], blocks[chunk][step], blocks[0][step]

    def with_bias(kernel, chunk, step, operands, outs, scratch, name, micros, after=(), specs=None, **options):
        fill = biases[step] is None
        body = functools.partial(kernel, fill=fill, chunk=chunk, step=step, **options, **common)
        operands = common_operands(chunk, step) + operands
        specs = specs or (WHOLE,) * len(outs)
        if not fill:
            return call(body, operands + (biases[step],), outs, scratch, name, micros, specs, after=after)
        *results, biases[step] = call(
            body, operands, outs + (bias_shape,), scratch, name, micros, specs + (WHOLE,), after=after
        )
        return results

    stats, final_stats = [None] * chunks, [None] * chunks
    sums, dq = [None] * chunks, [None] * chunks
    for chunk in each:
        after = [blocks[chunk - 1][1]] if chunk else []
        (stats[chunk],) = with_bias(
            stats_kernel, chunk, 0, (), (stats_shape,), [], "stats_own", 0.8, after
        )
    for step in range(1, reach):
        for chunk in each:
            here, stats[chunk] = lax.optimization_barrier((blocks[chunk][step], stats[chunk]))
            blocks[chunk].append(moved(here, up(step + 1)))
        for chunk in each:
            (stats[chunk],) = with_bias(
                stats_kernel, chunk, step, (stats[chunk],), (stats_shape,), [], "stats", 1.1
            )
    finished, returning, query_grad = [None] * chunks, [], []
    own_outs = (kv_grad_shape, jax.ShapeDtypeStruct(queries.shape, jnp.bfloat16))
    own_specs = (WHOLE, ANYWHERE)
    written_scratch = [
        pltpu.VMEM((rows, per_kv * HEAD_SIZE), jnp.bfloat16),
        pltpu.SemaphoreType.DMA((per_kv // 2,)),
    ]
    own_scratch = [turned] + written_scratch

    def far_grads(chunk, before):
        operands = (stats[chunk],)
        outs, specs, scratch = (finals_shape, sent_shape, dq_shape), (WHOLE,) * 3, [turned, total_sum]
        early_own = chunk == 0
        if early_own:
            operands += (own[chunk], blocks[0][1], biases[0])
            outs, specs, scratch = outs + own_outs, specs + own_specs, scratch + written_scratch
        final_stats[chunk], sums[chunk], dq[chunk], *rest = with_bias(
            far_kernel, chunk, reach, operands, outs, scratch, "grads_far", 1.3, before, specs,
            early_own=early_own, scale=scale,
        )
        if early_own:
            finished[chunk] = rest[0]
            query_grad.append(rest[1])
        return [sums[chunk]]

    def block_grads(chunk, step, before):
        early_own = step == 1 and chunk == 0 and chunks > 1
        body = functools.partial(
            grads_kernel, early_own=early_own, chunk=chunk, step=step, scale=scale, **common
        )
        operands = common_operands(chunk, step) + (final_stats[chunk], dq[chunk], biases[step])
        outs, specs, scratch, into = (kv_grad_shape, dq_shape), (WHOLE,) * 2, [turned], []
        if early_own:
            operands += (own[chunk + 1], final_stats[chunk + 1], dq[chunk + 1], biases[0])
            outs, specs, scratch = outs + own_outs, specs + own_specs, own_scratch
            into = [(query_grad.pop(), 3)]
        mine[chunk], dq[chunk], *rest = call(
            body, operands, outs, scratch, "grads", 1.6, specs, into=into, after=before
        )
        if early_own:
            finished[chunk + 1] = rest[0]
            query_grad.append(rest[1])
        return [mine[chunk]]

    def own_grads(chunk):
        done_before = finished[chunk] is not None
        body = functools.partial(own_kernel, done_before=done_before, chunk=chunk, scale=scale, **common)
        into = [(query_grad.pop(), 1)] if query_grad else []
        seen = 1 if done_before else 0
        finished[chunk], written = call(
            body,
            (queries, out_grad, own[0], blocks[chunk][0], blocks[0][seen])
            + (final_stats[chunk], dq[chunk], biases[0])
            + ((finished[chunk],) if done_before else ()),
            own_outs,
            own_scratch,
            "grads_own",
            1.8,
            out_specs=own_specs,
            into=into,
            after=[sums[chunk]],
        )
        query_grad.append(written)

    mine = [None] * chunks
    before = [stats[-1]]
    for chunk in each:
        before = far_grads(chunk, before)
    for step in range(reach - 1, 0, -1):
        arriving = [moved(sums[chunk], down(step + 1)) for chunk in each]
        for chunk in each:
            before = block_grads(chunk, step, before)
        arriving[0], mine[-1] = lax.optimization_barrier((arriving[0], mine[-1]))
        for chunk in each:
            here = arriving[chunk]
            if step == 1 and chunk:
                own_grads(chunk - 1)
                here, finished[chunk - 1] = lax.optimization_barrier((here, finished[chunk - 1]))
            sums[chunk] = (mine[chunk] + here.astype(jnp.float32)).astype(jnp.bfloat16)
            if step == 1:
                returning.append(moved(sums[chunk], down(1)))
    if reach == 1:
        returning += [moved(sums[chunk], down(1)) for chunk in each]
    for chunk in each if reach == 1 else each[-1:]:
        own_grads(chunk)

    returning[0], finished[-1] = lax.optimization_barrier((returning[0], finished[-1]))
    kv_swap = [(0, 1), (1, 0)]
    if chunks * lax.axis_size("kv") * HEAD_SIZE > key_matrix.shape[1]:
        key_scale = jnp.where(jnp.arange(2 * rows)[:, None] < rows, scale, 1.0).astype(jnp.float32)
        both = []
        for chunk in each:
            mine = (finished[chunk] + returning[chunk].astype(jnp.float32)).astype(jnp.bfloat16)
            other = lax.ppermute(mine, "kv", kv_swap).astype(jnp.float32)
            both.append(((mine.astype(jnp.float32) + other) * key_scale).astype(jnp.bfloat16))
        both = joined(both, 1)
        return query_grad[0], both[:rows], both[rows:]
    kv_grads, before = (), []
    for chunk in each:
        mine = call(
            functools.partial(finish_kernel, scale=scale),
            (finished[chunk], returning[chunk]),
            (sent_shape,),
            [],
            "finish",
            0.1,
            after=before,
        )[0]
        before = [mine]
        other = lax.ppermute(mine, "kv", kv_swap)
        kv_grads = pl.pallas_call(
            functools.partial(place_kernel, chunk=chunk, chunks=chunks),
            out_shape=(jax.ShapeDtypeStruct(key_matrix.shape, jnp.bfloat16),) * 2,
            in_specs=[WHOLE] * 2 + [ANYWHERE] * len(kv_grads),
            out_specs=(ANYWHERE,) * 2,
            scratch_shapes=[pltpu.SemaphoreType.DMA((2, 2))],
            input_output_aliases={2 + index: index for index in range(len(kv_grads))},
            compiler_params=pltpu.CompilerParams(vmem_limit_bytes=VMEM_LIMIT),
            name="place",
        )(mine, other, *kv_grads)
    return (query_grad[0], *kv_grads)


def solution(mesh):
    return jax.shard_map(
        shards,
        mesh=mesh,
        in_specs=(
            P(("groups", "ctx"), ("tp", "kv")),
            P(("groups", "ctx"), "tp"),
            P(("groups", "ctx"), "tp"),
            P(("groups", "ctx"), ("tp", "kv")),
            P(("groups", "ctx")),
        ),
        out_specs=(
            P(("groups", "ctx"), ("tp", "kv")),
            P(("groups", "ctx"), "tp"),
            P(("groups", "ctx"), "tp"),
        ),
        check_vma=False,
    )
```

```python
import functools
import jax
import jax.numpy as jnp
from jax import lax
from jax.experimental import pallas as pl
from jax.experimental.pallas import tpu as pltpu
from jax.sharding import PartitionSpec as P

QUERY_HEADS = 64
KEY_VALUE_HEADS = 8
HEAD_SIZE = 128
SEGMENT_ROWS = 16
TILE = 32
HINT = 0.2
AHEAD = 3
FILL_LOW = -1e30
LOG2_E = 1.4426950408889634
VMEM_LIMIT = 40 * 1024 * 1024
PACK_VMEM_LIMIT = 53 * 1024 * 1024 + 512 * 1024
LOAD_VMEM_LIMIT = 51 * 1024 * 1024
NUMBER_VMEM_LIMIT = 50 * 1024 * 1024
LOAD_PIECES = 8

WHOLE = pl.BlockSpec(memory_space=pltpu.VMEM)
ANYWHERE = pl.BlockSpec(memory_space=pl.ANY)


def across(a, b):
    return lax.dot_general(a, b, (((1,), (1,)), ((), ())), preferred_element_type=jnp.float32)


def times(a, b):
    return jnp.dot(a, b, preferred_element_type=jnp.float32)


def joined(pieces, axis):
    return pieces[0] if len(pieces) == 1 else jnp.concatenate(pieces, axis=axis)


def pack_kernel(k_ref, v_ref, *refs, first_of):
    *out_refs, sems = refs
    rows = k_ref.shape[0]
    first = first_of(lax.axis_index("kv"))
    copies = []
    for chunk, out_ref in enumerate(out_refs):
        columns = pl.ds(pl.multiple_of((first + chunk) * HEAD_SIZE, HEAD_SIZE), HEAD_SIZE)
        for part, ref in enumerate((k_ref, v_ref)):
            copies.append(
                pltpu.make_async_copy(
                    ref.at[:, columns],
                    out_ref.at[pl.ds(part * rows, rows), :],
                    sems.at[2 * chunk + part],
                )
            )
    for copy in copies:
        copy.start()
    for copy in copies:
        copy.wait()


def number_kernel(seg_ref, own_ref, out_ref):
    rows = seg_ref.shape[1]
    numbers = jnp.broadcast_to(seg_ref[...].astype(jnp.float32) + 1.0, (number_rows(rows), rows))
    pieces = [numbers[:, at : at + HEAD_SIZE] for at in range(0, rows, HEAD_SIZE)]
    tail = joined(pieces, 0).astype(jnp.bfloat16)
    out_ref[: 2 * rows, :] = own_ref[: 2 * rows, :]
    out_ref[pl.ds(2 * rows, tail.shape[0]), :] = tail


def load_kernel(q_ref, g_ref, own_ref, q_out_ref, g_out_ref, sems):
    pieces = sems.shape[1]
    count = q_ref.shape[0] // pieces
    copies = []
    for piece in range(pieces):
        here = slice(piece * count, (piece + 1) * count)
        for part, (ref, out_ref) in enumerate(((q_ref, q_out_ref), (g_ref, g_out_ref))):
            copies.append(
                pltpu.make_async_copy(
                    ref.at[here, :], out_ref.at[here, :], sems.at[part, piece]
                )
            )
    for copy in copies:
        copy.start()
    for copy in copies:
        copy.wait()


def number_rows(rows):
    return max(SEGMENT_ROWS * HEAD_SIZE // rows, 1)


def segment_row(ref, rows):
    repeat = number_rows(rows)
    count = repeat * rows // HEAD_SIZE
    tail = ref[pl.ds(ref.shape[0] - count, count), :].astype(jnp.float32)
    return joined([tail[at : at + 1] for at in range(0, tail.shape[0], repeat)], 1)


def fill_bias(bias_ref, own_ref, kv_ref, step):
    rows = bias_ref.shape[0]
    q_seg = segment_row(own_ref, rows)
    k_seg = segment_row(kv_ref, rows)
    k_col = jnp.broadcast_to(k_seg, (8, rows)).T[:, :1]
    allowed = k_col == q_seg
    if step == 0:
        k_pos = lax.broadcasted_iota(jnp.int32, (rows, rows), 0)
        q_pos = lax.broadcasted_iota(jnp.int32, (rows, rows), 1)
        allowed = allowed & (k_pos <= q_pos)
    bias_ref[...] = jnp.where(allowed, 0.0, FILL_LOW)


def activity(own_ref, kv_ref, step, rows):
    q_seg = segment_row(own_ref, rows)
    k_seg = segment_row(kv_ref, rows)
    reached = lax.axis_index("ctx") >= step
    first = q_seg[0, 0]
    return reached & (k_seg[0, rows - 1] >= first), k_seg[0, rows // 2 - 1] >= first


def full_units(per_kv, rows):
    return [(slice(0, rows), [(head, slice(0, rows))]) for head in range(per_kv)]


def own_units(per_kv, rows):
    half = rows // 2
    units = []
    for head in range(0, per_kv, 2):
        units += [(slice(0, half), [(head + i, slice(0, rows))]) for i in range(2)]
        units.append((slice(half, rows), [(head + i, slice(half, rows)) for i in range(2)]))
    return units


def late_units(per_kv, rows):
    return [(slice(rows // 2, rows), [(head, slice(0, rows))]) for head in range(per_kv)]


def early_units(per_kv, rows):
    early = slice(0, rows // 2)
    return [(slice(0, rows), [(head, early), (head + 1, early)]) for head in range(0, per_kv, 2)]


class Unit:
    def __init__(self, unit, base, q_ref, g_ref, kv_ref, bias_ref):
        self.keys, self.parts = unit
        self.rows = kv_ref.shape[0] // 2
        self.bias_ref = bias_ref
        rows = bias_ref.shape[0]
        self.q = self.gather(q_ref, base)
        self.g = self.gather(g_ref, base)
        k = kv_ref[self.keys, :]
        v = kv_ref[slice(rows + self.keys.start, rows + self.keys.stop), :]
        self.raw = across(k, self.q)
        self.dprobs = across(v, self.g)

    def gather(self, ref, base):
        return joined(
            [ref[span, (base + head) * HEAD_SIZE : (base + head + 1) * HEAD_SIZE] for head, span in self.parts],
            0,
        )

    def row(self, ref, part):
        return joined([ref[part, head : head + 1, span] for head, span in self.parts], 1)

    def put_row(self, ref, part, value):
        for (head, span), piece in zip(self.parts, self.split(value)):
            ref[part, head : head + 1, span] = piece

    def split(self, value):
        at, pieces = 0, []
        for _, span in self.parts:
            width = span.stop - span.start
            pieces.append(value[:, at : at + width])
            at += width
        return pieces

    def tiles(self):
        for first in range(0, self.keys.stop - self.keys.start, TILE):
            here = slice(first, first + TILE)
            key_rows = slice(self.keys.start + first, self.keys.start + first + TILE)
            bias = joined([self.bias_ref[key_rows, span] for _, span in self.parts], 1)
            yield bias, self.raw[here], self.dprobs[here]

    def updated(self, stats, factor):
        scores, top = [], None
        for bias, raw, _ in self.tiles():
            scores.append(raw * factor + bias)
            top = scores[-1] if top is None else jnp.maximum(top, scores[-1])
        peak = jnp.max(top, axis=0, keepdims=True)
        if stats is not None:
            peak = jnp.maximum(peak, stats[0])
        weights, total, weighted = [], None, None
        for tile, (_, _, dprobs) in zip(scores, self.tiles()):
            weights.append(jnp.exp2(tile - peak))
            product = weights[-1] * dprobs
            total = weights[-1] if total is None else total + weights[-1]
            weighted = product if weighted is None else weighted + product
        total = jnp.sum(total, axis=0, keepdims=True)
        weighted = jnp.sum(weighted, axis=0, keepdims=True)
        if stats is not None:
            fade = jnp.exp2(stats[0] - peak)
            total = total + stats[1] * fade
            weighted = weighted + stats[2] * fade
        return (peak, total, weighted), weights

    def lowered(self, log_total, delta, factor, weights=None, inverse=None):
        probs, dscores = [], []
        for index, (bias, raw, dprobs) in enumerate(self.tiles()):
            if weights is None:
                tile = jnp.exp2(raw * factor + bias - log_total)
            else:
                tile = weights[index] * inverse
            probs.append(tile.astype(jnp.bfloat16))
            dscores.append((tile * (dprobs - delta)).astype(jnp.bfloat16))
        self.probs, self.dscores = joined(probs, 0), joined(dscores, 0)


def in_turn(units, make, handle, count):
    made = [make(unit) for unit in units[:count]]
    for index in range(len(units)):
        if index + count < len(units):
            made.append(make(units[index + count]))
        handle(made[index])
        made[index] = None


class GradSum:
    def __init__(self, acc_ref, rows):
        self.acc_ref, self.rows, self.waiting, self.seen = acc_ref, rows, {}, set()

    def add(self, unit):
        key = unit.keys.start, unit.keys.stop
        self.waiting.setdefault(key, []).append(unit)
        if len(self.waiting[key]) == 4:
            self.flush(key)

    def flush(self, key):
        units = self.waiting.pop(key)
        first, last = key
        for offset, lhs, rhs in (
            (0, joined([u.dscores for u in units], 1), joined([u.q for u in units], 0)),
            (self.rows, joined([u.probs for u in units], 1), joined([u.g for u in units], 0)),
        ):
            here = slice(offset + first, offset + last)
            term = times(lhs, rhs)
            self.acc_ref[here, :] = self.acc_ref[here, :] + term if key in self.seen else term
        self.seen.add(key)

    def finish(self):
        for key in list(self.waiting):
            self.flush(key)


def finals(stats):
    return stats[0] + jnp.log2(stats[1]), stats[2] / stats[1]


def stats_kernel(ins, outs, scratch, *, early_own, fill, chunk, per_kv, factor, scale, step):
    q_ref, g_ref, own_seg_ref, kv_ref, kv_seg_ref = ins[:5]
    in_ref = ins[5] if step else None
    out_ref = outs[0]
    bias_ref = outs[-1] if fill else ins[-1]
    rows = q_ref.shape[0]

    def run():
        if fill:
            fill_bias(bias_ref, own_seg_ref, kv_seg_ref, step)

        def handle(unit):
            source = in_ref
            if step == 0:
                source = out_ref if unit.keys.start > 0 else None
            stats = None if source is None else tuple(unit.row(source, part) for part in range(3))
            for part, value in enumerate(unit.updated(stats, factor)[0]):
                unit.put_row(out_ref, part, value)

        units = full_units(per_kv, rows) if step else own_units(per_kv, rows)
        in_turn(units, lambda unit: Unit(unit, chunk * per_kv, q_ref, g_ref, kv_ref, bias_ref), handle, AHEAD)

    def own_early():
        near_seg_ref, own_kv_ref, stats_ref, own_bias_ref = ins[-5:-1]
        final_ref = scratch[0]
        for part, value in enumerate(finals((stats_ref[0], stats_ref[1], stats_ref[2]))):
            final_ref[part] = value
        own_run(
            (q_ref, g_ref, own_kv_ref, final_ref, None, own_bias_ref), outs[1:3], scratch[1:],
            early_own, per_kv, factor, scale,
        )

    if step == 0:
        run()
        if early_own is not None:
            near, _ = activity(own_seg_ref, ins[-5], 1, rows)
            pl.when(jnp.logical_not(near))(own_early)
        return
    active, _ = activity(own_seg_ref, kv_seg_ref, step, rows)
    pl.when(active)(run)

    @pl.when(jnp.logical_not(active))
    def _():
        out_ref[...] = in_ref[...]
        if early_own is not None:
            own_early()


def far_kernel(ins, outs, scratch, *, fill, chunk, per_kv, factor, step):
    q_ref, g_ref, own_seg_ref, kv_ref, kv_seg_ref, in_ref = ins[:6]
    out_ref, kv_grad_ref, dq_ref = outs[:3]
    bias_ref = outs[-1] if fill else ins[-1]
    kt_ref, acc_ref = scratch[:2]
    rows = q_ref.shape[0]
    half = rows // 2
    active, early = activity(own_seg_ref, kv_seg_ref, step, rows)
    log_total, delta = finals((in_ref[0], in_ref[1], in_ref[2]))
    out_ref[0] = log_total
    out_ref[1] = delta

    def run(units, keys):
        if fill:
            fill_bias(bias_ref, own_seg_ref, kv_seg_ref, step)
        kt_ref[...] = kv_ref[:rows, :].T
        if keys.start > 0:
            for offset in (0, rows):
                acc_ref[offset : offset + keys.start, :] = jnp.zeros((keys.start, HEAD_SIZE), jnp.float32)
        grads = GradSum(acc_ref, rows)

        def first(unit):
            stats = tuple(unit.row(in_ref, part) for part in range(3))
            stats, unit.weights = unit.updated(stats, factor)
            unit.finals = finals(stats)
            unit.inverse = 1.0 / stats[1]
            unit.put_row(out_ref, 0, unit.finals[0])
            unit.put_row(out_ref, 1, unit.finals[1])

        def second(unit):
            unit.lowered(*unit.finals, factor, unit.weights, unit.inverse)
            grads.add(unit)
            dq = times(kt_ref[:, unit.keys], unit.dscores)
            for (head, span), piece in zip(unit.parts, unit.split(dq)):
                dq_ref[head, :, span] = piece
                if span.stop < rows:
                    dq_ref[head, :, span.stop :] = jnp.zeros((HEAD_SIZE, rows - span.stop), jnp.float32)

        def both(unit):
            first(unit)
            second(unit)

        def make(unit):
            return Unit(unit, chunk * per_kv, q_ref, g_ref, kv_ref, bias_ref)

        if chunk % 2:
            made = []
            in_turn(units, make, lambda unit: (first(unit), made.append(unit)), AHEAD)
            for unit in made:
                second(unit)
        else:
            in_turn(units, make, both, AHEAD)
        grads.finish()
        kv_grad_ref[...] = acc_ref[...].astype(kv_grad_ref.dtype)

    @pl.when(active & jnp.logical_not(early))
    def _():
        run(late_units(per_kv, rows), slice(half, rows))

    @pl.when(active & early)
    def _():
        run(early_units(per_kv, rows), slice(0, rows))

    @pl.when(jnp.logical_not(active))
    def _():
        dq_ref[...] = jnp.zeros_like(dq_ref)
        kv_grad_ref[...] = jnp.zeros_like(kv_grad_ref)


def grads_kernel(ins, outs, scratch, *, chunk, per_kv, factor, step):
    q_ref, g_ref, own_seg_ref, kv_ref, kv_seg_ref, in_ref, dq_in_ref, bias_ref = ins
    kv_grad_ref, dq_ref = outs
    kt_ref = scratch[0]
    rows = q_ref.shape[0]

    def make(unit):
        return Unit(unit, chunk * per_kv, q_ref, g_ref, kv_ref, bias_ref)

    def run():
        kt_ref[...] = kv_ref[:rows, :].T
        grads = GradSum(kv_grad_ref, rows)

        def handle(unit):
            unit.lowered(unit.row(in_ref, 0), unit.row(in_ref, 1), factor)
            grads.add(unit)
            head = unit.parts[0][0]
            dq_ref[head] = dq_in_ref[head] + times(kt_ref[:, unit.keys], unit.dscores)

        in_turn(full_units(per_kv, rows), make, handle, AHEAD)
        grads.finish()

    active, _ = activity(own_seg_ref, kv_seg_ref, step, rows)
    pl.when(active)(run)

    @pl.when(jnp.logical_not(active))
    def _():
        kv_grad_ref[...] = jnp.zeros_like(kv_grad_ref)
        dq_ref[...] = dq_in_ref[...]


def own_run(ins, outs, scratch, chunk, per_kv, factor, scale):
    q_ref, g_ref, kv_ref, in_ref, dq_in_ref, bias_ref = ins
    kv_grad_ref, query_grad_ref = outs
    kt_ref, turned_ref, sems = scratch
    rows = q_ref.shape[0]
    half = rows // 2
    kt_ref[...] = kv_ref[:rows, :].T
    grads = GradSum(kv_grad_ref, rows)
    dq_now, copies = {}, []

    def send(head, count):
        here = slice(head * HEAD_SIZE, (head + count) * HEAD_SIZE)
        there = slice((chunk * per_kv + head) * HEAD_SIZE, (chunk * per_kv + head + count) * HEAD_SIZE)
        copies.append(
            pltpu.make_async_copy(turned_ref.at[:, here], query_grad_ref.at[:, there], sems.at[head // count])
        )
        copies[-1].start()

    def handle(unit):
        unit.lowered(unit.row(in_ref, 0), unit.row(in_ref, 1), factor)
        grads.add(unit)
        dq = times(kt_ref[:, unit.keys], unit.dscores)
        head = unit.parts[0][0]
        if unit.keys.start == 0:
            dq_now[head] = dq if dq_in_ref is None else dq_in_ref[head] + dq
            return
        for (other, _), piece in zip(unit.parts, unit.split(dq)):
            total = dq_now.pop(other)
            for at, value in ((0, total[:, :half]), (half, total[:, half:] + piece)):
                turned_ref[at : at + half, other * HEAD_SIZE : (other + 1) * HEAD_SIZE] = (
                    (value * scale).astype(jnp.bfloat16).T
                )
        send(head, len(unit.parts))

    def make(unit):
        return Unit(unit, chunk * per_kv, q_ref, g_ref, kv_ref, bias_ref)

    in_turn(own_units(per_kv, rows), make, handle, AHEAD)
    grads.finish()
    for copy in copies:
        copy.wait()


def own_kernel(ins, outs, scratch, *, done_before, chunk, per_kv, factor, scale):
    q_ref, g_ref, own_seg_ref, kv_ref, kv_seg_ref, in_ref, dq_in_ref, bias_ref = ins[:8]

    def run():
        own_run(
            (q_ref, g_ref, kv_ref, in_ref, dq_in_ref, bias_ref), outs, scratch,
            chunk, per_kv, factor, scale,
        )

    if not done_before:
        run()
        return
    active, _ = activity(own_seg_ref, kv_seg_ref, 1, q_ref.shape[0])
    pl.when(active)(run)

    @pl.when(jnp.logical_not(active))
    def _():
        outs[0][...] = ins[8][...]


def finish_kernel(ins, outs, _, *, scale):
    own_ref, arrived_ref = ins
    rows = own_ref.shape[0] // 2
    for first, factor in ((0, scale), (rows, 1.0)):
        here = slice(first, first + rows)
        total = (own_ref[here, :] + arrived_ref[here, :].astype(jnp.float32)) * factor
        outs[0][here, :] = total.astype(jnp.bfloat16)


def place_kernel(mine_ref, other_ref, *refs, chunk, chunks):
    *out_refs, sems = refs[-3:]
    rows = out_refs[0].shape[0]
    core = lax.axis_index("kv")
    copies = []
    for place, ref in enumerate((mine_ref, other_ref)):
        first = ((1 - core if place else core) * chunks + chunk) * HEAD_SIZE
        columns = pl.ds(pl.multiple_of(first, HEAD_SIZE), HEAD_SIZE)
        for part, out_ref in enumerate(out_refs):
            copies.append(
                pltpu.make_async_copy(
                    ref.at[pl.ds(part * rows, rows), :], out_ref.at[:, columns], sems.at[place, part]
                )
            )
    for copy in copies:
        copy.start()
    for copy in copies:
        copy.wait()


def shards(queries, key_matrix, value_matrix, out_grad, segments):
    rows = queries.shape[0]
    heads = queries.shape[1] // HEAD_SIZE
    group_width = QUERY_HEADS // KEY_VALUE_HEADS
    chunks = max(heads // group_width, 1)
    per_kv = heads // chunks
    ctx = lax.axis_size("ctx")
    groups = lax.axis_size("groups")
    longest = rows * ctx // 2
    reach = min(ctx - 1, (longest - 1 + rows - 1) // rows)
    scale = HEAD_SIZE ** (-0.5)
    factor = scale * LOG2_E
    tail = number_rows(rows) * rows // HEAD_SIZE
    block_shapes = tuple(
        jax.ShapeDtypeStruct((2 * rows + (0 if chunk else tail), HEAD_SIZE), jnp.bfloat16)
        for chunk in range(chunks)
    )
    pairs = per_kv * rows * rows
    each = range(chunks)

    def first_of(kv_index):
        return kv_index * heads // group_width

    def up(step):
        route = []
        for group in range(groups):
            at = group * ctx
            beside = (group + 1) % groups * ctx
            route += [(at + i, beside + i) for i in range(step - 1)]
            route += [(at + i, at + i + 1) for i in range(step - 1, ctx - 1)]
            route.append((at + ctx - 1, at + step - 1))
        return route

    def down(step):
        return [(target, source) for source, target in up(step)]

    def moved(array, route):
        return lax.ppermute(array, ("groups", "ctx"), route)

    def call(body, operands, outs, scratch, name, micros, out_specs=None, into=(), after=()):
        count = len(operands)
        extra = [array for array, _ in into] + list(after)
        specs = [out_specs[index] for _, index in into] + [ANYWHERE] * len(after)

        def kernel(*refs):
            rest = refs[count + len(extra) :]
            body(refs[:count], rest[: len(outs)], rest[len(outs) :])

        return pl.pallas_call(
            kernel,
            out_shape=outs,
            in_specs=[WHOLE] * count + specs,
            out_specs=out_specs or (WHOLE,) * len(outs),
            scratch_shapes=scratch,
            input_output_aliases={count + place: index for place, (_, index) in enumerate(into)},
            compiler_params=pltpu.CompilerParams(vmem_limit_bytes=VMEM_LIMIT),
            cost_estimate=pl.CostEstimate(
                flops=int(1153e6 * micros * HINT), bytes_accessed=4 * pairs // rows, transcendentals=pairs
            ),
            name=name,
        )(*operands, *extra)

    own = pl.pallas_call(
        functools.partial(pack_kernel, first_of=first_of),
        out_shape=block_shapes,
        in_specs=[ANYWHERE] * 2,
        out_specs=(WHOLE,) * chunks,
        scratch_shapes=[pltpu.SemaphoreType.DMA((2 * chunks,))],
        compiler_params=pltpu.CompilerParams(vmem_limit_bytes=PACK_VMEM_LIMIT),
        cost_estimate=pl.CostEstimate(flops=0, bytes_accessed=4 * 1024 * 1024, transcendentals=0),
        name="pack",
    )(key_matrix, value_matrix)
    own = list(own)
    own[0] = pl.pallas_call(
        number_kernel,
        out_shape=block_shapes[0],
        in_specs=[WHOLE] * 2,
        out_specs=WHOLE,
        input_output_aliases={1: 0},
        compiler_params=pltpu.CompilerParams(vmem_limit_bytes=NUMBER_VMEM_LIMIT),
        name="number",
    )(segments.reshape(1, rows), own[0])

    rows_shape = jax.ShapeDtypeStruct(queries.shape, jnp.bfloat16)
    queries, out_grad = pl.pallas_call(
        load_kernel,
        out_shape=(rows_shape, rows_shape),
        in_specs=[ANYWHERE] * 3,
        out_specs=(WHOLE, WHOLE),
        scratch_shapes=[pltpu.SemaphoreType.DMA((2, LOAD_PIECES))],
        compiler_params=pltpu.CompilerParams(vmem_limit_bytes=LOAD_VMEM_LIMIT),
        name="load",
    )(queries, out_grad, own[0])

    turned = pltpu.VMEM((HEAD_SIZE, rows), jnp.bfloat16)
    total_sum = pltpu.VMEM((2 * rows, HEAD_SIZE), jnp.float32)
    bias_shape = jax.ShapeDtypeStruct((rows, rows), jnp.float32)
    stats_shape = jax.ShapeDtypeStruct((3, per_kv, rows), jnp.float32)
    finals_shape = jax.ShapeDtypeStruct((2, per_kv, rows), jnp.float32)
    dq_shape = jax.ShapeDtypeStruct((per_kv, HEAD_SIZE, rows), jnp.float32)
    kv_grad_shape = jax.ShapeDtypeStruct((2 * rows, HEAD_SIZE), jnp.float32)
    sent_shape = jax.ShapeDtypeStruct((2 * rows, HEAD_SIZE), jnp.bfloat16)
    common = {"per_kv": per_kv, "factor": factor}
    biases = [None] * (reach + 1)
    own = list(lax.optimization_barrier(tuple(own)))
    blocks = [[own[chunk], moved(own[chunk], up(1))] for chunk in each]

    def common_operands(chunk, step):
        return queries, out_grad, own[0], blocks[chunk][step], blocks[0][step]

    def with_bias(
        kernel, chunk, step, operands, outs, scratch, name, micros, after=(), specs=None, into=(), **options
    ):
        fill = biases[step] is None
        body = functools.partial(kernel, fill=fill, chunk=chunk, step=step, **options, **common)
        operands = common_operands(chunk, step) + operands
        specs = specs or (WHOLE,) * len(outs)
        if not fill:
            return call(body, operands + (biases[step],), outs, scratch, name, micros, specs, into, after)
        *results, biases[step] = call(
            body, operands, outs + (bias_shape,), scratch, name, micros, specs + (WHOLE,), into, after
        )
        return results

    stats, final_stats = [None] * chunks, [None] * chunks
    sums, dq = [None] * chunks, [None] * chunks
    finished, returning, query_grad = [None] * chunks, [], []
    own_outs = (kv_grad_shape, jax.ShapeDtypeStruct(queries.shape, jnp.bfloat16))
    own_specs = (WHOLE, ANYWHERE)
    own_scratch = [
        turned,
        pltpu.VMEM((rows, per_kv * HEAD_SIZE), jnp.bfloat16),
        pltpu.SemaphoreType.DMA((per_kv // 2,)),
    ]

    def block_stats(chunk, step, early_own=None, after=()):
        operands = () if step == 0 else (stats[chunk],)
        outs, specs, scratch, into = (stats_shape,), (WHOLE,), [], []
        if early_own is not None:
            operands += (blocks[0][1], own[early_own], stats[early_own], biases[0])
            outs, specs = outs + own_outs, specs + own_specs
            scratch = [pltpu.VMEM(finals_shape.shape, jnp.float32)] + own_scratch
            into = [(query_grad.pop(), 2)] if query_grad else []
        stats[chunk], *rest = with_bias(
            stats_kernel, chunk, step, operands, outs, scratch, "stats" if step else "stats_own", 1.0,
            after, specs, into, early_own=early_own, scale=scale,
        )
        if early_own is not None:
            finished[early_own] = rest[0]
            query_grad.append(rest[1])

    early = chunks > 1 and reach > 1
    for chunk in each:
        after = [blocks[chunk - 1][1]] if chunk else []
        block_stats(chunk, 0, 0 if early and chunk == 1 else None, after)
    for step in range(1, reach):
        for chunk in each:
            here, stats[chunk] = lax.optimization_barrier((blocks[chunk][step], stats[chunk]))
            blocks[chunk].append(moved(here, up(step + 1)))
        for chunk in each:
            block_stats(chunk, step, 1 if early and step == 1 and chunk == 1 else None)

    def far_grads(chunk, before):
        final_stats[chunk], sums[chunk], dq[chunk] = with_bias(
            far_kernel, chunk, reach, (stats[chunk],), (finals_shape, sent_shape, dq_shape),
            [turned, total_sum], "grads_far", 1.3, before,
        )
        return [sums[chunk]]

    def block_grads(chunk, step, before):
        body = functools.partial(grads_kernel, chunk=chunk, step=step, **common)
        operands = common_operands(chunk, step) + (final_stats[chunk], dq[chunk], biases[step])
        mine[chunk], dq[chunk] = call(
            body, operands, (kv_grad_shape, dq_shape), [turned], "grads", 1.6, after=before
        )
        return [mine[chunk]]

    def own_grads(chunk):
        done_before = finished[chunk] is not None
        body = functools.partial(own_kernel, done_before=done_before, chunk=chunk, scale=scale, **common)
        into = [(query_grad.pop(), 1)] if query_grad else []
        seen = 1 if done_before else 0
        finished[chunk], written = call(
            body,
            (queries, out_grad, own[0], blocks[chunk][0], blocks[0][seen])
            + (final_stats[chunk], dq[chunk], biases[0])
            + ((finished[chunk],) if done_before else ()),
            own_outs,
            own_scratch,
            "grads_own",
            1.8,
            out_specs=own_specs,
            into=into,
            after=[sums[chunk]],
        )
        query_grad.append(written)

    mine = [None] * chunks
    before = [stats[-1]]
    for chunk in each:
        before = far_grads(chunk, before)
    for step in range(reach - 1, 0, -1):
        arriving = [moved(sums[chunk], down(step + 1)) for chunk in each]
        for chunk in each:
            before = block_grads(chunk, step, before)
        arriving[0], mine[-1] = lax.optimization_barrier((arriving[0], mine[-1]))
        for chunk in each:
            here = arriving[chunk]
            if step == 1 and chunk:
                own_grads(chunk - 1)
                here, finished[chunk - 1] = lax.optimization_barrier((here, finished[chunk - 1]))
            sums[chunk] = (mine[chunk] + here.astype(jnp.float32)).astype(jnp.bfloat16)
            if step == 1:
                returning.append(moved(sums[chunk], down(1)))
    if reach == 1:
        returning += [moved(sums[chunk], down(1)) for chunk in each]
    for chunk in each if reach == 1 else each[-1:]:
        own_grads(chunk)

    returning[0], finished[-1] = lax.optimization_barrier((returning[0], finished[-1]))
    kv_swap = [(0, 1), (1, 0)]
    if chunks * lax.axis_size("kv") * HEAD_SIZE > key_matrix.shape[1]:
        key_scale = jnp.where(jnp.arange(2 * rows)[:, None] < rows, scale, 1.0).astype(jnp.float32)
        both = []
        for chunk in each:
            mine = (finished[chunk] + returning[chunk].astype(jnp.float32)).astype(jnp.bfloat16)
            other = lax.ppermute(mine, "kv", kv_swap).astype(jnp.float32)
            both.append(((mine.astype(jnp.float32) + other) * key_scale).astype(jnp.bfloat16))
        both = joined(both, 1)
        return query_grad[0], both[:rows], both[rows:]
    kv_grads, before = (), []
    for chunk in each:
        mine = call(
            functools.partial(finish_kernel, scale=scale),
            (finished[chunk], returning[chunk]),
            (sent_shape,),
            [],
            "finish",
            0.1,
            after=before,
        )[0]
        before = [mine]
        other = lax.ppermute(mine, "kv", kv_swap)
        kv_grads = pl.pallas_call(
            functools.partial(place_kernel, chunk=chunk, chunks=chunks),
            out_shape=(jax.ShapeDtypeStruct(key_matrix.shape, jnp.bfloat16),) * 2,
            in_specs=[WHOLE] * 2 + [ANYWHERE] * len(kv_grads),
            out_specs=(ANYWHERE,) * 2,
            scratch_shapes=[pltpu.SemaphoreType.DMA((2, 2))],
            input_output_aliases={2 + index: index for index in range(len(kv_grads))},
            compiler_params=pltpu.CompilerParams(vmem_limit_bytes=VMEM_LIMIT),
            name="place",
        )(mine, other, *kv_grads)
    return (query_grad[0], *kv_grads)


def solution(mesh):
    return jax.shard_map(
        shards,
        mesh=mesh,
        in_specs=(
            P(("groups", "ctx"), ("tp", "kv")),
            P(("groups", "ctx"), "tp"),
            P(("groups", "ctx"), "tp"),
            P(("groups", "ctx"), ("tp", "kv")),
            P(("groups", "ctx")),
        ),
        out_specs=(
            P(("groups", "ctx"), ("tp", "kv")),
            P(("groups", "ctx"), "tp"),
            P(("groups", "ctx"), "tp"),
        ),
        check_vma=False,
    )
```

```python
import functools
import jax
import jax.numpy as jnp
from jax import lax
from jax.experimental import pallas as pl
from jax.experimental.pallas import tpu as pltpu
from jax.sharding import PartitionSpec as P

QUERY_HEADS = 64
KEY_VALUE_HEADS = 8
HEAD_SIZE = 128
SEGMENT_ROWS = 16
TILE = 32
HINT = 0.2
AHEAD = 3
FILL_LOW = -1e30
LOG2_E = 1.4426950408889634
VMEM_LIMIT = 40 * 1024 * 1024
PACK_VMEM_LIMIT = 53 * 1024 * 1024 + 512 * 1024
LOAD_VMEM_LIMIT = 51 * 1024 * 1024
NUMBER_VMEM_LIMIT = 50 * 1024 * 1024
LOAD_PIECES = 8

WHOLE = pl.BlockSpec(memory_space=pltpu.VMEM)
ANYWHERE = pl.BlockSpec(memory_space=pl.ANY)


def across(a, b):
    return lax.dot_general(a, b, (((1,), (1,)), ((), ())), preferred_element_type=jnp.float32)


def times(a, b):
    return jnp.dot(a, b, preferred_element_type=jnp.float32)


def joined(pieces, axis):
    return pieces[0] if len(pieces) == 1 else jnp.concatenate(pieces, axis=axis)


def pack_kernel(k_ref, v_ref, *refs, first_of):
    *out_refs, sems = refs
    rows = k_ref.shape[0]
    first = first_of(lax.axis_index("kv"))
    copies = []
    for chunk, out_ref in enumerate(out_refs):
        columns = pl.ds(pl.multiple_of((first + chunk) * HEAD_SIZE, HEAD_SIZE), HEAD_SIZE)
        for part, ref in enumerate((k_ref, v_ref)):
            copies.append(
                pltpu.make_async_copy(
                    ref.at[:, columns],
                    out_ref.at[pl.ds(part * rows, rows), :],
                    sems.at[2 * chunk + part],
                )
            )
    for copy in copies:
        copy.start()
    for copy in copies:
        copy.wait()


def number_kernel(seg_ref, own_ref, out_ref):
    rows = seg_ref.shape[1]
    numbers = jnp.broadcast_to(seg_ref[...].astype(jnp.float32) + 1.0, (number_rows(rows), rows))
    pieces = [numbers[:, at : at + HEAD_SIZE] for at in range(0, rows, HEAD_SIZE)]
    tail = joined(pieces, 0).astype(jnp.bfloat16)
    out_ref[: 2 * rows, :] = own_ref[: 2 * rows, :]
    out_ref[pl.ds(2 * rows, tail.shape[0]), :] = tail


def load_kernel(q_ref, g_ref, own_ref, q_out_ref, g_out_ref, sems):
    pieces = sems.shape[1]
    count = q_ref.shape[0] // pieces
    copies = []
    for piece in range(pieces):
        here = slice(piece * count, (piece + 1) * count)
        for part, (ref, out_ref) in enumerate(((q_ref, q_out_ref), (g_ref, g_out_ref))):
            copies.append(
                pltpu.make_async_copy(
                    ref.at[here, :], out_ref.at[here, :], sems.at[part, piece]
                )
            )
    for copy in copies:
        copy.start()
    for copy in copies:
        copy.wait()


def number_rows(rows):
    return max(SEGMENT_ROWS * HEAD_SIZE // rows, 1)


def segment_row(ref, rows):
    repeat = number_rows(rows)
    count = repeat * rows // HEAD_SIZE
    tail = ref[pl.ds(ref.shape[0] - count, count), :].astype(jnp.float32)
    return joined([tail[at : at + 1] for at in range(0, tail.shape[0], repeat)], 1)


def fill_bias(bias_ref, own_ref, kv_ref, step):
    rows = bias_ref.shape[0]
    q_seg = segment_row(own_ref, rows)
    k_seg = segment_row(kv_ref, rows)
    k_col = jnp.broadcast_to(k_seg, (8, rows)).T[:, :1]
    allowed = k_col == q_seg
    if step == 0:
        k_pos = lax.broadcasted_iota(jnp.int32, (rows, rows), 0)
        q_pos = lax.broadcasted_iota(jnp.int32, (rows, rows), 1)
        allowed = allowed & (k_pos <= q_pos)
    bias_ref[...] = jnp.where(allowed, 0.0, FILL_LOW)


def activity(own_ref, kv_ref, step, rows):
    q_seg = segment_row(own_ref, rows)
    k_seg = segment_row(kv_ref, rows)
    reached = lax.axis_index("ctx") >= step
    first = q_seg[0, 0]
    return reached & (k_seg[0, rows - 1] >= first), k_seg[0, rows // 2 - 1] >= first


def full_units(per_kv, rows):
    return [(slice(0, rows), [(head, slice(0, rows))]) for head in range(per_kv)]


def own_units(per_kv, rows):
    half = rows // 2
    units = []
    for head in range(0, per_kv, 2):
        units += [(slice(0, half), [(head + i, slice(0, rows))]) for i in range(2)]
        units.append((slice(half, rows), [(head + i, slice(half, rows)) for i in range(2)]))
    return units


def late_units(per_kv, rows):
    return [(slice(rows // 2, rows), [(head, slice(0, rows))]) for head in range(per_kv)]


def early_units(per_kv, rows):
    early = slice(0, rows // 2)
    return [(slice(0, rows), [(head, early), (head + 1, early)]) for head in range(0, per_kv, 2)]


class Unit:
    def __init__(self, unit, base, q_ref, g_ref, kv_ref, bias_ref):
        self.keys, self.parts = unit
        self.rows = kv_ref.shape[0] // 2
        self.bias_ref = bias_ref
        rows = bias_ref.shape[0]
        self.q = self.gather(q_ref, base)
        self.g = self.gather(g_ref, base)
        k = kv_ref[self.keys, :]
        v = kv_ref[slice(rows + self.keys.start, rows + self.keys.stop), :]
        self.raw = across(k, self.q)
        self.dprobs = across(v, self.g)

    def gather(self, ref, base):
        return joined(
            [ref[span, (base + head) * HEAD_SIZE : (base + head + 1) * HEAD_SIZE] for head, span in self.parts],
            0,
        )

    def row(self, ref, part):
        return joined([ref[part, head : head + 1, span] for head, span in self.parts], 1)

    def put_row(self, ref, part, value):
        for (head, span), piece in zip(self.parts, self.split(value)):
            ref[part, head : head + 1, span] = piece

    def split(self, value):
        at, pieces = 0, []
        for _, span in self.parts:
            width = span.stop - span.start
            pieces.append(value[:, at : at + width])
            at += width
        return pieces

    def tiles(self):
        for first in range(0, self.keys.stop - self.keys.start, TILE):
            here = slice(first, first + TILE)
            key_rows = slice(self.keys.start + first, self.keys.start + first + TILE)
            bias = joined([self.bias_ref[key_rows, span] for _, span in self.parts], 1)
            yield bias, self.raw[here], self.dprobs[here]

    def updated(self, stats, factor):
        scores, top = [], None
        for bias, raw, _ in self.tiles():
            scores.append(raw * factor + bias)
            top = scores[-1] if top is None else jnp.maximum(top, scores[-1])
        peak = jnp.max(top, axis=0, keepdims=True)
        if stats is not None:
            peak = jnp.maximum(peak, stats[0])
        weights, total, weighted = [], None, None
        for tile, (_, _, dprobs) in zip(scores, self.tiles()):
            weights.append(jnp.exp2(tile - peak))
            product = weights[-1] * dprobs
            total = weights[-1] if total is None else total + weights[-1]
            weighted = product if weighted is None else weighted + product
        total = jnp.sum(total, axis=0, keepdims=True)
        weighted = jnp.sum(weighted, axis=0, keepdims=True)
        if stats is not None:
            fade = jnp.exp2(stats[0] - peak)
            total = total + stats[1] * fade
            weighted = weighted + stats[2] * fade
        return (peak, total, weighted), weights

    def lowered(self, log_total, delta, factor, weights=None, inverse=None):
        probs, dscores = [], []
        for index, (bias, raw, dprobs) in enumerate(self.tiles()):
            if weights is None:
                tile = jnp.exp2(raw * factor + bias - log_total)
            else:
                tile = weights[index] * inverse
            probs.append(tile.astype(jnp.bfloat16))
            dscores.append((tile * (dprobs - delta)).astype(jnp.bfloat16))
        self.probs, self.dscores = joined(probs, 0), joined(dscores, 0)


def in_turn(units, make, handle, count):
    made = [make(unit) for unit in units[:count]]
    for index in range(len(units)):
        if index + count < len(units):
            made.append(make(units[index + count]))
        handle(made[index])
        made[index] = None


class GradSum:
    def __init__(self, acc_ref, rows):
        self.acc_ref, self.rows, self.waiting, self.seen = acc_ref, rows, {}, set()

    def add(self, unit):
        key = unit.keys.start, unit.keys.stop
        self.waiting.setdefault(key, []).append(unit)
        if len(self.waiting[key]) == 4:
            self.flush(key)

    def flush(self, key):
        units = self.waiting.pop(key)
        first, last = key
        for offset, lhs, rhs in (
            (0, joined([u.dscores for u in units], 1), joined([u.q for u in units], 0)),
            (self.rows, joined([u.probs for u in units], 1), joined([u.g for u in units], 0)),
        ):
            here = slice(offset + first, offset + last)
            term = times(lhs, rhs)
            self.acc_ref[here, :] = self.acc_ref[here, :] + term if key in self.seen else term
        self.seen.add(key)

    def finish(self):
        for key in list(self.waiting):
            self.flush(key)


def finals(stats):
    return stats[0] + jnp.log2(stats[1]), stats[2] / stats[1]


def stats_kernel(ins, outs, scratch, *, early_own, fill, chunk, per_kv, factor, scale, step):
    q_ref, g_ref, own_seg_ref, kv_ref, kv_seg_ref = ins[:5]
    in_ref = ins[5] if step else None
    out_ref = outs[0]
    bias_ref = outs[-1] if fill else ins[-1]
    rows = q_ref.shape[0]

    def run():
        if fill:
            fill_bias(bias_ref, own_seg_ref, kv_seg_ref, step)

        def handle(unit):
            source = in_ref
            if step == 0:
                source = out_ref if unit.keys.start > 0 else None
            stats = None if source is None else tuple(unit.row(source, part) for part in range(3))
            for part, value in enumerate(unit.updated(stats, factor)[0]):
                unit.put_row(out_ref, part, value)

        units = full_units(per_kv, rows) if step else own_units(per_kv, rows)
        in_turn(units, lambda unit: Unit(unit, chunk * per_kv, q_ref, g_ref, kv_ref, bias_ref), handle, AHEAD)

    def own_early():
        near_seg_ref, own_kv_ref, stats_ref, own_bias_ref = ins[-5:-1]
        final_ref = scratch[0]
        for part, value in enumerate(finals((stats_ref[0], stats_ref[1], stats_ref[2]))):
            final_ref[part] = value
        own_run(
            (q_ref, g_ref, own_kv_ref, final_ref, (), own_bias_ref), outs[1:3], scratch[1:],
            early_own, per_kv, factor, scale,
        )

    if step == 0:
        run()
        if early_own is not None:
            near, _ = activity(own_seg_ref, ins[-5], 1, rows)
            pl.when(jnp.logical_not(near))(own_early)
        return
    active, _ = activity(own_seg_ref, kv_seg_ref, step, rows)
    pl.when(active)(run)

    @pl.when(jnp.logical_not(active))
    def _():
        out_ref[...] = in_ref[...]
        if early_own is not None:
            own_early()


def far_kernel(ins, outs, scratch, *, fill, chunk, per_kv, factor, step):
    q_ref, g_ref, own_seg_ref, kv_ref, kv_seg_ref, in_ref = ins[:6]
    out_ref, kv_grad_ref, dq_ref = outs[:3]
    bias_ref = outs[-1] if fill else ins[-1]
    kt_ref, acc_ref = scratch[:2]
    rows = q_ref.shape[0]
    half = rows // 2
    active, early = activity(own_seg_ref, kv_seg_ref, step, rows)
    log_total, delta = finals((in_ref[0], in_ref[1], in_ref[2]))
    out_ref[0] = log_total
    out_ref[1] = delta

    def run(units, keys):
        if fill:
            fill_bias(bias_ref, own_seg_ref, kv_seg_ref, step)
        kt_ref[...] = kv_ref[:rows, :].T
        if keys.start > 0:
            for offset in (0, rows):
                acc_ref[offset : offset + keys.start, :] = jnp.zeros((keys.start, HEAD_SIZE), jnp.float32)
        grads = GradSum(acc_ref, rows)

        def first(unit):
            stats = tuple(unit.row(in_ref, part) for part in range(3))
            stats, unit.weights = unit.updated(stats, factor)
            unit.finals = finals(stats)
            unit.inverse = 1.0 / stats[1]
            unit.put_row(out_ref, 0, unit.finals[0])
            unit.put_row(out_ref, 1, unit.finals[1])

        def second(unit):
            unit.lowered(*unit.finals, factor, unit.weights, unit.inverse)
            grads.add(unit)
            dq = times(kt_ref[:, unit.keys], unit.dscores)
            for (head, span), piece in zip(unit.parts, unit.split(dq)):
                dq_ref[head, :, span] = piece
                if span.stop < rows:
                    dq_ref[head, :, span.stop :] = jnp.zeros((HEAD_SIZE, rows - span.stop), jnp.float32)

        def both(unit):
            first(unit)
            second(unit)

        def make(unit):
            return Unit(unit, chunk * per_kv, q_ref, g_ref, kv_ref, bias_ref)

        if chunk % 2:
            made = []
            in_turn(units, make, lambda unit: (first(unit), made.append(unit)), AHEAD)
            for unit in made:
                second(unit)
        else:
            in_turn(units, make, both, AHEAD)
        grads.finish()
        kv_grad_ref[...] = acc_ref[...].astype(kv_grad_ref.dtype)

    @pl.when(active & jnp.logical_not(early))
    def _():
        run(late_units(per_kv, rows), slice(half, rows))

    @pl.when(active & early)
    def _():
        run(early_units(per_kv, rows), slice(0, rows))

    @pl.when(jnp.logical_not(active))
    def _():
        dq_ref[...] = jnp.zeros_like(dq_ref)
        kv_grad_ref[...] = jnp.zeros_like(kv_grad_ref)


def grads_kernel(ins, outs, scratch, *, chunk, per_kv, factor, step):
    q_ref, g_ref, own_seg_ref, kv_ref, kv_seg_ref, in_ref, *dq_in_refs, bias_ref = ins
    kv_grad_ref, dq_ref = outs
    kt_ref = scratch[0]
    rows = q_ref.shape[0]

    def make(unit):
        return Unit(unit, chunk * per_kv, q_ref, g_ref, kv_ref, bias_ref)

    def run():
        kt_ref[...] = kv_ref[:rows, :].T
        grads = GradSum(kv_grad_ref, rows)

        def handle(unit):
            unit.lowered(unit.row(in_ref, 0), unit.row(in_ref, 1), factor)
            grads.add(unit)
            head = unit.parts[0][0]
            dq = times(kt_ref[:, unit.keys], unit.dscores)
            dq_ref[head] = dq_in_refs[0][head] + dq if dq_in_refs else dq

        in_turn(full_units(per_kv, rows), make, handle, AHEAD)
        grads.finish()

    active, _ = activity(own_seg_ref, kv_seg_ref, step, rows)
    pl.when(active)(run)

    @pl.when(jnp.logical_not(active))
    def _():
        kv_grad_ref[...] = jnp.zeros_like(kv_grad_ref)
        dq_ref[...] = dq_in_refs[0][...] if dq_in_refs else jnp.zeros_like(dq_ref)


def own_run(ins, outs, scratch, chunk, per_kv, factor, scale):
    q_ref, g_ref, kv_ref, in_ref, dq_in_refs, bias_ref = ins
    kv_grad_ref, query_grad_ref = outs
    kt_ref, turned_ref, sems = scratch
    rows = q_ref.shape[0]
    half = rows // 2
    kt_ref[...] = kv_ref[:rows, :].T
    grads = GradSum(kv_grad_ref, rows)
    dq_now, copies = {}, []

    def send(head, count):
        here = slice(head * HEAD_SIZE, (head + count) * HEAD_SIZE)
        there = slice((chunk * per_kv + head) * HEAD_SIZE, (chunk * per_kv + head + count) * HEAD_SIZE)
        copies.append(
            pltpu.make_async_copy(turned_ref.at[:, here], query_grad_ref.at[:, there], sems.at[head // count])
        )
        copies[-1].start()

    def handle(unit):
        unit.lowered(unit.row(in_ref, 0), unit.row(in_ref, 1), factor)
        grads.add(unit)
        dq = times(kt_ref[:, unit.keys], unit.dscores)
        head = unit.parts[0][0]
        if unit.keys.start == 0:
            for ref in dq_in_refs:
                dq = dq + ref[head]
            dq_now[head] = dq
            return
        for (other, _), piece in zip(unit.parts, unit.split(dq)):
            total = dq_now.pop(other)
            for at, value in ((0, total[:, :half]), (half, total[:, half:] + piece)):
                turned_ref[at : at + half, other * HEAD_SIZE : (other + 1) * HEAD_SIZE] = (
                    (value * scale).astype(jnp.bfloat16).T
                )
        send(head, len(unit.parts))

    def make(unit):
        return Unit(unit, chunk * per_kv, q_ref, g_ref, kv_ref, bias_ref)

    in_turn(own_units(per_kv, rows), make, handle, AHEAD)
    grads.finish()
    for copy in copies:
        copy.wait()


def own_kernel(ins, outs, scratch, *, terms, done_before, chunk, per_kv, factor, scale):
    q_ref, g_ref, own_seg_ref, kv_ref, kv_seg_ref, in_ref = ins[:6]
    dq_in_refs, bias_ref = ins[6 : 6 + terms], ins[6 + terms]

    def run():
        own_run(
            (q_ref, g_ref, kv_ref, in_ref, dq_in_refs, bias_ref), outs, scratch,
            chunk, per_kv, factor, scale,
        )

    if not done_before:
        run()
        return
    active, _ = activity(own_seg_ref, kv_seg_ref, 1, q_ref.shape[0])
    pl.when(active)(run)

    @pl.when(jnp.logical_not(active))
    def _():
        outs[0][...] = ins[7 + terms][...]


def finish_kernel(ins, outs, _, *, scale):
    own_ref, arrived_ref = ins
    rows = own_ref.shape[0] // 2
    for first, factor in ((0, scale), (rows, 1.0)):
        here = slice(first, first + rows)
        total = (own_ref[here, :] + arrived_ref[here, :].astype(jnp.float32)) * factor
        outs[0][here, :] = total.astype(jnp.bfloat16)


def place_kernel(mine_ref, other_ref, *refs, chunk, chunks):
    *out_refs, sems = refs[-3:]
    rows = out_refs[0].shape[0]
    core = lax.axis_index("kv")
    copies = []
    for place, ref in enumerate((mine_ref, other_ref)):
        first = ((1 - core if place else core) * chunks + chunk) * HEAD_SIZE
        columns = pl.ds(pl.multiple_of(first, HEAD_SIZE), HEAD_SIZE)
        for part, out_ref in enumerate(out_refs):
            copies.append(
                pltpu.make_async_copy(
                    ref.at[pl.ds(part * rows, rows), :], out_ref.at[:, columns], sems.at[place, part]
                )
            )
    for copy in copies:
        copy.start()
    for copy in copies:
        copy.wait()


def shards(queries, key_matrix, value_matrix, out_grad, segments):
    rows = queries.shape[0]
    heads = queries.shape[1] // HEAD_SIZE
    group_width = QUERY_HEADS // KEY_VALUE_HEADS
    chunks = max(heads // group_width, 1)
    per_kv = heads // chunks
    ctx = lax.axis_size("ctx")
    groups = lax.axis_size("groups")
    longest = rows * ctx // 2
    reach = min(ctx - 1, (longest - 1 + rows - 1) // rows)
    scale = HEAD_SIZE ** (-0.5)
    factor = scale * LOG2_E
    tail = number_rows(rows) * rows // HEAD_SIZE
    block_shapes = tuple(
        jax.ShapeDtypeStruct((2 * rows + (0 if chunk else tail), HEAD_SIZE), jnp.bfloat16)
        for chunk in range(chunks)
    )
    pairs = per_kv * rows * rows
    each = range(chunks)

    def first_of(kv_index):
        return kv_index * heads // group_width

    def up(step):
        route = []
        for group in range(groups):
            at = group * ctx
            beside = (group + 1) % groups * ctx
            route += [(at + i, beside + i) for i in range(step - 1)]
            route += [(at + i, at + i + 1) for i in range(step - 1, ctx - 1)]
            route.append((at + ctx - 1, at + step - 1))
        return route

    def down(step):
        return [(target, source) for source, target in up(step)]

    def moved(array, route):
        return lax.ppermute(array, ("groups", "ctx"), route)

    def call(body, operands, outs, scratch, name, micros, out_specs=None, into=(), after=(), same=()):
        count = len(operands)
        extra = [array for array, _ in into] + list(after)
        specs = [out_specs[index] for _, index in into] + [ANYWHERE] * len(after)

        def kernel(*refs):
            rest = refs[count + len(extra) :]
            body(refs[:count], rest[: len(outs)], rest[len(outs) :])

        return pl.pallas_call(
            kernel,
            out_shape=outs,
            in_specs=[WHOLE] * count + specs,
            out_specs=out_specs or (WHOLE,) * len(outs),
            scratch_shapes=scratch,
            input_output_aliases={count + place: index for place, (_, index) in enumerate(into)} | dict(same),
            compiler_params=pltpu.CompilerParams(vmem_limit_bytes=VMEM_LIMIT),
            cost_estimate=pl.CostEstimate(
                flops=int(1153e6 * micros * HINT), bytes_accessed=4 * pairs // rows, transcendentals=pairs
            ),
            name=name,
        )(*operands, *extra)

    own = pl.pallas_call(
        functools.partial(pack_kernel, first_of=first_of),
        out_shape=block_shapes,
        in_specs=[ANYWHERE] * 2,
        out_specs=(WHOLE,) * chunks,
        scratch_shapes=[pltpu.SemaphoreType.DMA((2 * chunks,))],
        compiler_params=pltpu.CompilerParams(vmem_limit_bytes=PACK_VMEM_LIMIT),
        cost_estimate=pl.CostEstimate(flops=0, bytes_accessed=4 * 1024 * 1024, transcendentals=0),
        name="pack",
    )(key_matrix, value_matrix)
    own = list(own)
    own[0] = pl.pallas_call(
        number_kernel,
        out_shape=block_shapes[0],
        in_specs=[WHOLE] * 2,
        out_specs=WHOLE,
        input_output_aliases={1: 0},
        compiler_params=pltpu.CompilerParams(vmem_limit_bytes=NUMBER_VMEM_LIMIT),
        name="number",
    )(segments.reshape(1, rows), own[0])

    rows_shape = jax.ShapeDtypeStruct(queries.shape, jnp.bfloat16)
    queries, out_grad = pl.pallas_call(
        load_kernel,
        out_shape=(rows_shape, rows_shape),
        in_specs=[ANYWHERE] * 3,
        out_specs=(WHOLE, WHOLE),
        scratch_shapes=[pltpu.SemaphoreType.DMA((2, LOAD_PIECES))],
        compiler_params=pltpu.CompilerParams(vmem_limit_bytes=LOAD_VMEM_LIMIT),
        name="load",
    )(queries, out_grad, own[0])

    turned = pltpu.VMEM((HEAD_SIZE, rows), jnp.bfloat16)
    total_sum = pltpu.VMEM((2 * rows, HEAD_SIZE), jnp.float32)
    bias_shape = jax.ShapeDtypeStruct((rows, rows), jnp.float32)
    stats_shape = jax.ShapeDtypeStruct((3, per_kv, rows), jnp.float32)
    finals_shape = jax.ShapeDtypeStruct((2, per_kv, rows), jnp.float32)
    dq_shape = jax.ShapeDtypeStruct((per_kv, HEAD_SIZE, rows), jnp.float32)
    kv_grad_shape = jax.ShapeDtypeStruct((2 * rows, HEAD_SIZE), jnp.float32)
    sent_shape = jax.ShapeDtypeStruct((2 * rows, HEAD_SIZE), jnp.bfloat16)
    common = {"per_kv": per_kv, "factor": factor}
    biases = [None] * (reach + 1)
    own = list(lax.optimization_barrier(tuple(own)))
    blocks = [[own[chunk], moved(own[chunk], up(1))] for chunk in each]

    def common_operands(chunk, step):
        return queries, out_grad, own[0], blocks[chunk][step], blocks[0][step]

    def with_bias(
        kernel, chunk, step, operands, outs, scratch, name, micros, after=(), specs=None, into=(), **options
    ):
        fill = biases[step] is None
        body = functools.partial(kernel, fill=fill, chunk=chunk, step=step, **options, **common)
        operands = common_operands(chunk, step) + operands
        specs = specs or (WHOLE,) * len(outs)
        if not fill:
            return call(body, operands + (biases[step],), outs, scratch, name, micros, specs, into, after)
        *results, biases[step] = call(
            body, operands, outs + (bias_shape,), scratch, name, micros, specs + (WHOLE,), into, after
        )
        return results

    stats, final_stats = [None] * chunks, [None] * chunks
    sums, dq = [None] * chunks, [None] * chunks
    finished, returning, query_grad = [None] * chunks, [], []
    own_outs = (kv_grad_shape, jax.ShapeDtypeStruct(queries.shape, jnp.bfloat16))
    own_specs = (WHOLE, ANYWHERE)
    own_scratch = [
        turned,
        pltpu.VMEM((rows, per_kv * HEAD_SIZE), jnp.bfloat16),
        pltpu.SemaphoreType.DMA((per_kv // 2,)),
    ]

    def block_stats(chunk, step, early_own=None, after=()):
        operands = () if step == 0 else (stats[chunk],)
        outs, specs, scratch, into = (stats_shape,), (WHOLE,), [], []
        if early_own is not None:
            operands += (blocks[0][1], own[early_own], stats[early_own], biases[0])
            outs, specs = outs + own_outs, specs + own_specs
            scratch = [pltpu.VMEM(finals_shape.shape, jnp.float32)] + own_scratch
            into = [(query_grad.pop(), 2)] if query_grad else []
        stats[chunk], *rest = with_bias(
            stats_kernel, chunk, step, operands, outs, scratch, "stats" if step else "stats_own", 1.0,
            after, specs, into, early_own=early_own, scale=scale,
        )
        if early_own is not None:
            finished[early_own] = rest[0]
            query_grad.append(rest[1])

    early = chunks > 1 and reach > 1
    for chunk in each:
        after = [blocks[chunk - 1][1]] if chunk else []
        block_stats(chunk, 0, 0 if early and chunk == 1 else None, after)
    for step in range(1, reach):
        for chunk in each:
            here, stats[chunk] = lax.optimization_barrier((blocks[chunk][step], stats[chunk]))
            blocks[chunk].append(moved(here, up(step + 1)))
        for chunk in each:
            block_stats(chunk, step, 1 if early and step == 1 and chunk == 1 else None)

    def far_grads(chunk, before):
        final_stats[chunk], sums[chunk], *dq[chunk] = with_bias(
            far_kernel, chunk, reach, (stats[chunk],), (finals_shape, sent_shape, dq_shape),
            [turned, total_sum], "grads_far", 1.3, before,
        )
        return [sums[chunk]]

    def block_grads(chunk, step, before):
        body = functools.partial(grads_kernel, chunk=chunk, step=step, **common)
        so_far = tuple(dq[chunk]) if step > 1 else ()
        operands = common_operands(chunk, step) + (final_stats[chunk],) + so_far + (biases[step],)
        mine[chunk], term = call(
            body, operands, (kv_grad_shape, dq_shape), [turned], "grads", 1.6, after=before
        )
        dq[chunk] = [term] if step > 1 else dq[chunk] + [term]
        return [mine[chunk]]

    def own_grads(chunk):
        done_before = finished[chunk] is not None
        body = functools.partial(
            own_kernel, terms=len(dq[chunk]), done_before=done_before, chunk=chunk, scale=scale, **common
        )
        into = [(query_grad.pop(), 1)] if query_grad else []
        seen = 1 if done_before else 0
        finished[chunk], written = call(
            body,
            (queries, out_grad, own[0], blocks[chunk][0], blocks[0][seen])
            + (final_stats[chunk], *dq[chunk], biases[0])
            + ((finished[chunk],) if done_before else ()),
            own_outs,
            own_scratch,
            "grads_own",
            1.8,
            out_specs=own_specs,
            into=into,
            after=[sums[chunk]],
        )
        query_grad.append(written)

    mine = [None] * chunks
    before = [stats[-1]]
    for chunk in each:
        before = far_grads(chunk, before)
    for step in range(reach - 1, 0, -1):
        arriving = [moved(sums[chunk], down(step + 1)) for chunk in each]
        for chunk in each:
            before = block_grads(chunk, step, before)
        arriving[0], mine[-1] = lax.optimization_barrier((arriving[0], mine[-1]))
        for chunk in each:
            here = arriving[chunk]
            if step == 1 and chunk:
                own_grads(chunk - 1)
                here, finished[chunk - 1] = lax.optimization_barrier((here, finished[chunk - 1]))
            sums[chunk] = (mine[chunk] + here.astype(jnp.float32)).astype(jnp.bfloat16)
            if step == 1:
                returning.append(moved(sums[chunk], down(1)))
    if reach == 1:
        returning += [moved(sums[chunk], down(1)) for chunk in each]
    for chunk in each if reach == 1 else each[-1:]:
        own_grads(chunk)

    returning[0], finished[-1] = lax.optimization_barrier((returning[0], finished[-1]))
    kv_swap = [(0, 1), (1, 0)]
    if chunks * lax.axis_size("kv") * HEAD_SIZE > key_matrix.shape[1]:
        key_scale = jnp.where(jnp.arange(2 * rows)[:, None] < rows, scale, 1.0).astype(jnp.float32)
        both = []
        for chunk in each:
            mine = (finished[chunk] + returning[chunk].astype(jnp.float32)).astype(jnp.bfloat16)
            other = lax.ppermute(mine, "kv", kv_swap).astype(jnp.float32)
            both.append(((mine.astype(jnp.float32) + other) * key_scale).astype(jnp.bfloat16))
        both = joined(both, 1)
        return query_grad[0], both[:rows], both[rows:]
    kv_grads, before = (), []
    for chunk in each:
        mine = call(
            functools.partial(finish_kernel, scale=scale),
            (finished[chunk], returning[chunk]),
            (sent_shape,),
            [],
            "finish",
            0.1,
            after=before,
        )[0]
        before = [mine]
        other = lax.ppermute(mine, "kv", kv_swap)
        kv_grads = pl.pallas_call(
            functools.partial(place_kernel, chunk=chunk, chunks=chunks),
            out_shape=(jax.ShapeDtypeStruct(key_matrix.shape, jnp.bfloat16),) * 2,
            in_specs=[WHOLE] * 2 + [ANYWHERE] * len(kv_grads),
            out_specs=(ANYWHERE,) * 2,
            scratch_shapes=[pltpu.SemaphoreType.DMA((2, 2))],
            input_output_aliases={2 + index: index for index in range(len(kv_grads))},
            compiler_params=pltpu.CompilerParams(vmem_limit_bytes=VMEM_LIMIT),
            name="place",
        )(mine, other, *kv_grads)
    return (query_grad[0], *kv_grads)


def solution(mesh):
    return jax.shard_map(
        shards,
        mesh=mesh,
        in_specs=(
            P(("groups", "ctx"), ("tp", "kv")),
            P(("groups", "ctx"), "tp"),
            P(("groups", "ctx"), "tp"),
            P(("groups", "ctx"), ("tp", "kv")),
            P(("groups", "ctx")),
        ),
        out_specs=(
            P(("groups", "ctx"), ("tp", "kv")),
            P(("groups", "ctx"), "tp"),
            P(("groups", "ctx"), "tp"),
        ),
        check_vma=False,
    )
```
